512 devices in a mesh: seq: 64 (over y, z), kv: 8 (over x, core).
Axes of the slice: x: 4, y: 4, z: 16, core: 2. Of those that a mesh axis runs over, the one named last changes fastest.
Arguments:
- q_heads: bfloat16 [16384, 64, 128], P(('seq', 'kv')), may hold values from -21 to 21
- k_heads: bfloat16 [16384, 8, 128], P(('seq', 'kv')), may hold values from -10 to 10
- v_heads: bfloat16 [16384, 8, 128], P(('seq', 'kv')), may hold values from -6 to 6
- d_out: bfloat16 [16384, 64, 128], P(('seq', 'kv')), may hold values from -6 to 6
- positions: int32 [16384], P(('seq', 'kv')), may hold values from 0 to 767, as said below
- subtree_end: int32 [16384], replicated, may hold values from 0 to 16383, as said below
- ancestors: int32 [128, 6], P('seq'), may hold values from -1 to 127, as said below
Outputs:
- attn_out: bfloat16 [16384, 64, 128], P(('seq', 'kv'))
- dq_grad: bfloat16 [16384, 64, 128], P(('seq', 'kv'))
- dk_grad: bfloat16 [16384, 8, 128], P(('seq', 'kv'))
- dv_grad: bfloat16 [16384, 8, 128], P(('seq', 'kv'))
The draws below stay inside these ranges and needn't reach their ends.
Inputs may be any that keep to these rules, and one draw needn't show every extreme that they name: `ancestors`: row b lists the blocks on the path from the root of b's prefix tree down to b itself, root first, then -1 to the end of the row. The blocks of one tree are consecutive, at most 15 of them, so every listed block lies in b - 14 to b. Tokens stand in depth-first order of a forest of prefix trees; key s is an ancestor of query t, or t itself, exactly when s <= t <= subtree_end[s]. The first token of every block is an ancestor of all later tokens of its block and of all tokens of the blocks below it. `positions`: each token's depth in its prefix tree, 0 at the first token of a tree.
All inputs are finite; a program needn't handle non-finite values.
Results may differ from the reference program's by a relative error of at most 0.02.
Values may be sent and summed in bfloat16 or wider, within the bound.
A program may use at most 64 MiB of HBM per device.

```python
import math
import jax
import jax.numpy as jnp
from jax import lax

HEADS = 64
KVH = 8
DH = 128
BLK = 128
ANC = 6
TOKENS = 16384
NBLK = 128
SPAN = 15


def build_tree(key):
    tree_key = jax.random.fold_in(key, 101)
    subkeys = jax.random.split(tree_key, 5)
    forced_start = jax.random.randint(subkeys[0], (), 0, NBLK - SPAN + 1)
    root_draw = jax.random.randint(subkeys[1], (NBLK,), 0, 100)
    depth_draw = jax.random.randint(subkeys[2], (NBLK,), 2, ANC + 1)
    trunk_len = jax.random.randint(subkeys[3], (NBLK,), 1, BLK // 2 + 1)
    block_index = jnp.arange(NBLK, dtype=jnp.int32)
    forced_offset = block_index - forced_start
    forced = (forced_offset >= 0) & (forced_offset < SPAN)
    side_len = jnp.where(forced, 0, jax.random.randint(subkeys[4], (NBLK,), 0, BLK // 2))
    split_pos = trunk_len + side_len
    slots = jnp.arange(ANC, dtype=jnp.int32) + 1

    def forward_step(loop_carry, inputs):
        depth_prev, group_len, path_blocks, path_tail = loop_carry
        this_block, this_offset, is_forced, root_value, depth_value, this_trunk, this_split = inputs
        new_root = (this_block == 0) | is_forced & (this_offset == 0) | ~is_forced & ((group_len >= SPAN) | (root_value < 15))
        free_depth = jnp.minimum(depth_value, depth_prev + 1)
        chosen = jnp.where(is_forced & (this_offset < ANC), this_offset + 1, free_depth)
        depth_now = jnp.where(new_root, 1, chosen).astype(jnp.int32)
        base_depth = jnp.where(new_root, 0, path_tail[depth_now - 1] + 1).astype(jnp.int32)
        tail_depth = base_depth + this_trunk + (BLK - 1) - this_split
        path_blocks = path_blocks.at[depth_now].set(this_block)
        path_tail = path_tail.at[depth_now].set(tail_depth)
        listed = jnp.where(slots <= depth_now, path_blocks[slots], -1).astype(jnp.int32)
        group_len = jnp.where(new_root, 1, group_len + 1).astype(jnp.int32)
        return ((depth_now, group_len, path_blocks, path_tail), (depth_now, base_depth, listed))
    start_carry = (jnp.int32(0), jnp.int32(0), jnp.zeros((ANC + 1,), jnp.int32), jnp.zeros((ANC + 1,), jnp.int32))
    _, (depths, base_depths, listed_rows) = lax.scan(forward_step, start_carry, (block_index, forced_offset, forced, root_draw, depth_draw, trunk_len, split_pos))

    def backward_step(nearest, inputs):
        this_block, depth_now = inputs
        levels = jnp.arange(ANC + 1, dtype=jnp.int32)
        last_block = jnp.min(jnp.where(levels <= depth_now, nearest, NBLK)) - 1
        nearest = nearest.at[depth_now].set(this_block)
        return (nearest, last_block.astype(jnp.int32))
    _, last_blocks = lax.scan(backward_step, jnp.full((ANC + 1,), NBLK, jnp.int32), (block_index, depths), reverse=True)
    inside = jnp.arange(BLK, dtype=jnp.int32)[None, :]
    trunk_col = trunk_len[:, None]
    split_col = split_pos[:, None]
    token_depth = base_depths[:, None] + jnp.where(inside < split_col, inside, trunk_col + inside - split_col)
    on_side = (inside >= trunk_col) & (inside < split_col)
    token_end = jnp.where(on_side, block_index[:, None] * BLK + split_col - 1, (last_blocks[:, None] + 1) * BLK - 1)
    return (token_depth.reshape(TOKENS).astype(jnp.int32), token_end.reshape(TOKENS).astype(jnp.int32), listed_rows)


def draw_positions(key, part):
    return build_tree(key)[0]


def draw_subtree_end(key, part):
    return build_tree(key)[1]


def draw_ancestors(key, part):
    return build_tree(key)[2]


def draw_q_heads(key, part):
    own_key = jax.random.fold_in(key, 11)
    subkeys = jax.random.split(own_key, 1)
    values = jnp.clip(jax.random.normal(subkeys[0], (TOKENS, HEADS, DH), jnp.float32), -6.0, 6.0)
    return values.astype(jnp.bfloat16)


def draw_k_heads(key, part):
    own_key = jax.random.fold_in(key, 13)
    subkeys = jax.random.split(own_key, 1)
    values = jnp.clip(jax.random.normal(subkeys[0], (TOKENS, KVH, DH), jnp.float32), -6.0, 6.0)
    return values.astype(jnp.bfloat16)


def level_of(key, dims, cuts, least, largest):
    factor_of = 1.0
    for position, parts in cuts:
        steps = jax.random.uniform(jax.random.fold_in(jax.random.fold_in(key, 6), position), (parts,), jnp.float32, least / len(cuts), largest / len(cuts))
        factor_of = factor_of * jnp.repeat(jnp.exp(steps), dims[position] // parts).reshape((-1,) + (1,) * (len(dims) - 1 - position))
    return factor_of


def scatter_about(key, shape, deviation, reach, pieces=(), kind=jnp.bfloat16):
    level = level_of(key, shape, pieces, -0.22, 0.18) if pieces else 1.0
    array = jax.random.normal(key, shape, jnp.float32) * deviation * level
    return jnp.minimum(jnp.maximum(array, -reach), reach).astype(kind)


def setup_inputs(seed: int = 0) -> dict:
    arg_keys = jax.random.split(jax.random.key(seed), 8)
    q_heads = draw_q_heads(jax.random.fold_in(arg_keys[7], 71), 0)
    k_heads = draw_k_heads(jax.random.fold_in(arg_keys[7], 71), 0)
    v_heads = scatter_about(arg_keys[2], (TOKENS, KVH, DH), 1.0, 6.0, ((0, 512),))
    d_out = scatter_about(arg_keys[3], (TOKENS, HEADS, DH), 1.0, 6.0, ((0, 512),))
    positions = draw_positions(jax.random.fold_in(arg_keys[7], 71), 0)
    subtree_end = draw_subtree_end(jax.random.fold_in(arg_keys[7], 71), 0)
    ancestors = draw_ancestors(jax.random.fold_in(arg_keys[7], 71), 0)
    return dict(q_heads=q_heads, k_heads=k_heads, v_heads=v_heads, d_out=d_out, positions=positions, subtree_end=subtree_end, ancestors=ancestors)


rope_base = 500000.0
masked_value = -1e+30

def rope_tables(positions, head_width):
    half_width = head_width // 2
    exponent = jnp.arange(half_width, dtype=jnp.float32) * (2.0 / head_width)
    frequency = jnp.power(jnp.float32(rope_base), -exponent)
    angle = positions.astype(jnp.float32)[:, None] * frequency[None, :]
    cosine = jnp.concatenate([jnp.cos(angle), jnp.cos(angle)], axis=1)[:, None, :]
    sine = jnp.concatenate([jnp.sin(angle), jnp.sin(angle)], axis=1)[:, None, :]
    return (cosine, sine)

def rotate_half(values):
    half_width = values.shape[-1] // 2
    return jnp.concatenate([-values[..., half_width:], values[..., :half_width]], axis=-1)

def rope_apply(values, cosine, sine):
    return values * cosine + rotate_half(values) * sine

def rope_back(values, cosine, sine):
    return values * cosine - rotate_half(values) * sine

def widen(values):
    return lax.optimization_barrier(values).astype(jnp.float32)

def product(form, left, right):
    return jnp.einsum(form, left.astype(jnp.float32), right.astype(jnp.float32), precision=lax.Precision.HIGHEST)

def reference(q_heads, k_heads, v_heads, d_out, positions, subtree_end, ancestors):
    head_width = q_heads.shape[2]
    group_size = HEADS // KVH
    score_scale = 1.0 / math.sqrt(head_width)
    cosine, sine = rope_tables(positions, head_width)
    q_rot = rope_apply(q_heads.astype(jnp.float32), cosine, sine).astype(jnp.bfloat16)
    k_rot = rope_apply(k_heads.astype(jnp.float32), cosine, sine).astype(jnp.bfloat16)
    query_blocks = widen(q_rot).reshape(NBLK, BLK, KVH, group_size, head_width)
    grad_blocks = d_out.astype(jnp.float32).reshape(NBLK, BLK, KVH, group_size, head_width)
    key_blocks = widen(k_rot).reshape(NBLK, BLK, KVH, head_width)
    value_blocks = v_heads.astype(jnp.float32).reshape(NBLK, BLK, KVH, head_width)
    end_blocks = subtree_end.reshape(NBLK, BLK)
    inside = jnp.arange(BLK, dtype=jnp.int32)

    def one_block(loop_carry, block_index):
        key_grad, value_grad = loop_carry
        listed = ancestors[block_index]
        valid = listed >= 0
        safe_block = jnp.where(valid, listed, 0).astype(jnp.int32)
        key_rows = key_blocks[safe_block].reshape(ANC * BLK, KVH, head_width)
        value_rows = value_blocks[safe_block].reshape(ANC * BLK, KVH, head_width)
        key_pos = (safe_block[:, None] * BLK + inside[None, :]).reshape(ANC * BLK)
        key_end = end_blocks[safe_block].reshape(ANC * BLK)
        key_valid = jnp.repeat(valid, BLK)
        query_pos = block_index * BLK + inside
        visible = key_valid[None, :] & (key_pos[None, :] <= query_pos[:, None]) & (query_pos[:, None] <= key_end[None, :])
        queries = query_blocks[block_index]
        grad_rows = grad_blocks[block_index]
        scores = product('tkgd,skd->kgts', queries, key_rows) * score_scale
        masked = jnp.where(visible, scores, masked_value)
        row_max = lax.optimization_barrier(jnp.max(masked, axis=-1))
        row_total = lax.optimization_barrier(jnp.sum(jnp.where(visible, jnp.exp(masked - row_max[..., None]), 0.0), axis=-1))
        log_total = row_max + jnp.log(row_total)
        probability = jnp.where(visible, jnp.exp(masked - log_total[..., None]), 0.0)
        probability_low = widen(probability.astype(jnp.bfloat16))
        attended = product('kgts,skd->tkgd', probability_low, value_rows).astype(jnp.bfloat16)
        inner_product = lax.optimization_barrier(jnp.sum(grad_rows * widen(attended), axis=-1))
        dprob = product('tkgd,skd->kgts', grad_rows, value_rows)
        dscore = probability * (dprob - jnp.transpose(inner_product, (1, 2, 0))[..., None]) * score_scale
        dscore_low = widen(dscore.astype(jnp.bfloat16))
        query_grad = product('kgts,skd->tkgd', dscore_low, key_rows).astype(jnp.bfloat16)
        key_part = product('kgts,tkgd->skd', dscore_low, queries).reshape(ANC, BLK, KVH, head_width)
        value_part = product('kgts,tkgd->skd', probability_low, grad_rows).reshape(ANC, BLK, KVH, head_width)
        key_grad = key_grad.at[safe_block].add(key_part)
        value_grad = value_grad.at[safe_block].add(value_part)
        return ((key_grad, value_grad), (attended, query_grad))
    empty_grad = jnp.zeros((NBLK, BLK, KVH, head_width), jnp.float32)
    (key_grad, value_grad), (attended, query_grad) = lax.scan(one_block, (empty_grad, empty_grad), jnp.arange(NBLK, dtype=jnp.int32))
    attn_out = attended.reshape(TOKENS, HEADS, head_width)
    dq_rot = query_grad.reshape(TOKENS, HEADS, head_width)
    dk_rot = key_grad.reshape(TOKENS, KVH, head_width).astype(jnp.bfloat16)
    dv_grad = value_grad.reshape(TOKENS, KVH, head_width).astype(jnp.bfloat16)
    dq_grad = rope_back(widen(dq_rot), cosine, sine).astype(jnp.bfloat16)
    dk_grad = rope_back(widen(dk_rot), cosine, sine).astype(jnp.bfloat16)
    return (attn_out, dq_grad, dk_grad, dv_grad)
```

```python
import functools
import math

import jax
import jax.numpy as jnp
from jax import lax
from jax.experimental import pallas as pl
from jax.experimental.pallas import tpu as pltpu
from jax.sharding import PartitionSpec as P

MESH = pl.DeviceIdType.MESH
BF16, F32 = jnp.bfloat16, jnp.float32
BLK = 128
ANC = 6
WIN = 7
KV = 8
GRP = 8
TOK = 32
DH = 128
ROWS = TOK * GRP
KEYS = ANC * BLK
ROPE_BASE = 500000.0
HIDDEN = -1e30
SCALE = 1.0 / math.sqrt(DH)
LOG2E = 1.4426950408889634
NT = (((1,), (1,)), ((), ()))
NN = (((1,), (0,)), ((), ()))


def dot(a, b, dims=NN):
    return lax.dot_general(a, b, dims, preferred_element_type=F32)


def kernel(
    lines,
    q_ref, k_ref, v_ref, g_ref, cos_ref, sin_ref, anc_ref, end_ref,
    o_out, dq_out, dk_out, dv_out,
    stage, ksend, vsend, qsend, gsend, qbuf, gbuf, kwin, vwin,
    kb, vb, kbt, vbt, bias, prob, plow, dka, dva,
    osend, dqsend, orecv, dqrecv, tmp, gout, gin, dksend, dvsend, dkrecv, dvrecv,
    in_s, in_r, win_s, win_r, grad_s, grad_r, out_s, out_r,
):
    s = lax.axis_index("seq")
    j = lax.axis_index("kv")
    left, right = s - 1, s + 1

    barrier = pltpu.get_barrier_semaphore()
    for p in range(1, KV):
        peer = lax.rem(j + p, KV)
        pl.semaphore_signal(barrier, inc=1, device_id=(s, peer), device_id_type=MESH)

    @pl.when(s > 0)
    def _():
        pl.semaphore_signal(barrier, inc=1, device_id=(left, j), device_id_type=MESH)

    @pl.when(s < lines - 1)
    def _():
        pl.semaphore_signal(barrier, inc=1, device_id=(right, j), device_id_type=MESH)

    cosine = cos_ref[...][:, None, :]
    sine = sin_ref[...][:, None, :]

    def rope(x):
        return x * cosine + pltpu.roll(x, DH // 2, 2) * sine

    def rope_back(x):
        return x * cosine - pltpu.roll(x, DH // 2, 2) * sine

    stage[...] = rope(k_ref[...].astype(F32)).reshape(ROWS, DH)
    for h in range(KV):
        ksend[h] = stage[pl.ds(h, TOK, stride=KV), :].astype(BF16)
    stage[...] = v_ref[...].astype(F32).reshape(ROWS, DH)
    for h in range(KV):
        vsend[h] = stage[pl.ds(h, TOK, stride=KV), :].astype(BF16)

    pl.semaphore_wait(
        barrier, KV - 1 + (s > 0).astype(jnp.int32) + (s < lines - 1).astype(jnp.int32)
    )

    def line_copy(kind, src, dst, peer, slot, sems):
        return pltpu.make_async_remote_copy(
            src_ref=src, dst_ref=dst, send_sem=sems[0].at[kind, peer],
            recv_sem=sems[1].at[kind, slot], device_id=(s, peer), device_id_type=MESH,
        )

    def own_rows(win):
        return win.at[j // 4, pl.ds(pl.multiple_of(lax.rem(j, 4) * TOK, TOK), TOK)]

    sends = ((ksend, kwin), (vsend, vwin))
    for kind, (src, win) in enumerate(sends):
        for p in range(1, KV):
            peer = lax.rem(j + p, KV)
            line_copy(kind, src.at[peer], own_rows(win), peer, j, (in_s, in_r)).start()
    kwin[j // 4, pl.ds(pl.multiple_of(lax.rem(j, 4) * TOK, TOK), TOK), :] = ksend[j]
    vwin[j // 4, pl.ds(pl.multiple_of(lax.rem(j, 4) * TOK, TOK), TOK), :] = vsend[j]

    for pair in range(KV // 2):
        x = q_ref[:, pair * 16:(pair + 1) * 16, :].astype(F32).reshape(TOK, 2, GRP, DH)
        y = g_ref[:, pair * 16:(pair + 1) * 16, :].astype(F32).reshape(TOK, 2, GRP, DH)
        for u in range(2):
            qsend[2 * pair + u] = rope(x[:, u]).reshape(ROWS, DH).astype(BF16)
            gsend[2 * pair + u] = y[:, u].reshape(ROWS, DH).astype(BF16)
    for p in range(1, KV):
        peer = lax.rem(j + p, KV)
        line_copy(2, qsend.at[peer], qbuf.at[j], peer, j, (in_s, in_r)).start()
        line_copy(3, gsend.at[peer], gbuf.at[j], peer, j, (in_s, in_r)).start()
    qbuf[j] = qsend[j]
    gbuf[j] = gsend[j]

    def arrived(kind, peer):
        pair = ((ksend.at[peer], own_rows(kwin)), (vsend.at[peer], own_rows(vwin)),
                (qsend.at[peer], qbuf.at[j]), (gsend.at[peer], gbuf.at[j]))[kind]
        line_copy(kind, pair[0], pair[1], peer, peer, (in_s, in_r)).wait_recv()

    def hop(which, d, h):
        win = (kwin, vwin)[which]
        return pltpu.make_async_remote_copy(
            src_ref=win.at[2 * (d - 1) + h], dst_ref=win.at[2 * d + h],
            send_sem=win_s.at[2 * which + h, d], recv_sem=win_r.at[2 * which + h, d],
            device_id=(right, j), device_id_type=MESH,
        )

    for which in range(2):
        for p in range(1, KV):
            arrived(which, lax.rem(j + p, KV))
    for d in range(1, WIN + 1):
        for which in range(2):
            for h in range(2):
                if d > 1:
                    @pl.when(s >= d - 1)
                    def _():
                        hop(which, d - 1, h).wait_recv()

                @pl.when((s >= d - 1) & (s < lines - 1))
                def _():
                    hop(which, d, h).start()
        if d == 1:
            def mask_step(u, carry):
                b = u // ANC
                slot = lax.rem(u, ANC)
                a = anc_ref[b, slot]
                row = end_ref[pl.ds(jnp.maximum(a, 0), 1), :].astype(F32)
                last = jnp.broadcast_to(row, (BLK, BLK)).T
                last = jnp.where(a >= 0, last, -1.0)
                first = (a * BLK + lax.broadcasted_iota(jnp.int32, (BLK, BLK), 0)).astype(F32)
                lane = lax.broadcasted_iota(jnp.int32, (BLK, BLK), 1) // GRP
                for c in range(4):
                    for half in range(2):
                        query = ((2 * s + b) * BLK + c * TOK + half * (TOK // 2) + lane).astype(F32)
                        seen = (query >= first) & (query <= last)
                        bias[4 * b + c, pl.ds(pl.multiple_of(slot * BLK, BLK), BLK),
                             half * BLK:(half + 1) * BLK] = jnp.where(seen, 0.0, HIDDEN)
                return carry

            lax.fori_loop(0, 2 * ANC, mask_step, 0)

    for which in range(2):
        for h in range(2):
            @pl.when(s >= WIN)
            def _():
                hop(which, WIN, h).wait_recv()

    def gather_step(u, carry):
        b = u // ANC
        slot = lax.rem(u, ANC)
        a = anc_ref[b, slot]
        index = 2 * (s - lax.shift_right_arithmetic(a, 1)) + (a & 1)
        index = jnp.where(a >= 0, jnp.clip(index, 0, 2 * WIN + 1), 0)
        rows = pl.ds(pl.multiple_of(slot * BLK, BLK), BLK)
        keys, values = kwin[index], vwin[index]
        kb[b, rows, :] = keys
        vb[b, rows, :] = values
        kbt[b, :, rows] = keys.astype(F32).T.astype(BF16)
        vbt[b, :, rows] = values.astype(F32).T.astype(BF16)
        return carry

    lax.fori_loop(0, 2 * ANC, gather_step, 0)

    for kind in (2, 3):
        for p in range(1, KV):
            arrived(kind, lax.rem(j + p, KV))

    dka[...] = jnp.zeros_like(dka)
    dva[...] = jnp.zeros_like(dva)

    def chunk(i, carry):
        b = i // 4
        queries, cotangent = qbuf[i], gbuf[i]
        scores = dot(kb[b], queries, NT) * (SCALE * LOG2E) + bias[i]
        top = jnp.max(scores, axis=0, keepdims=True)
        p = jnp.exp2(scores - top)
        p = p * (1.0 / jnp.sum(p, axis=0, keepdims=True))
        low = p.astype(BF16)
        mine = pl.ds(b * ANC, ANC)
        dva[mine] += dot(low, cotangent).reshape(ANC, BLK, DH)
        attended = dot(vbt[b], low).astype(BF16)
        osend[i] = attended.astype(F32).T.astype(BF16)
        inner = jnp.sum(cotangent.astype(F32).T * attended.astype(F32), axis=0, keepdims=True)
        dprob = dot(vb[b], cotangent, NT)
        dscore = (p * (dprob - inner) * SCALE).astype(BF16)
        dka[mine] += dot(dscore, queries).reshape(ANC, BLK, DH)
        dqsend[i] = dot(kbt[b], dscore).T.astype(BF16)

        @pl.when(i != j)
        def _():
            line_copy(0, osend.at[i], orecv.at[j], i, j, (out_s, out_r)).start()
            line_copy(1, dqsend.at[i], dqrecv.at[j], i, j, (out_s, out_r)).start()

        @pl.when(i == j)
        def _():
            orecv[j] = osend[i]
            dqrecv[j] = dqsend[i]

        return carry

    lax.fori_loop(0, KV, chunk, 0)

    def back(which, d, h):
        return pltpu.make_async_remote_copy(
            src_ref=gout.at[which, 2 * d + h], dst_ref=gin.at[which, 2 * (d - 1) + h],
            send_sem=grad_s.at[2 * which + h, d], recv_sem=grad_r.at[2 * which + h, d - 1],
            device_id=(left, j), device_id_type=MESH,
        )

    def place(b, block):
        index = 2 * ANC
        for slot in range(ANC):
            hit = (anc_ref[b, slot] == block) & (block >= 0)
            index = jnp.where(hit, b * ANC + slot, index)
        return index

    for d in range(WIN, -1, -1):
        for h in range(2):
            block = 2 * (s - d) + h
            first, second = place(0, block), place(1, block)
            for which in range(2):
                acc = (dka, dva)[which]
                tmp[which, h] = acc[first] + acc[second]
        for which in range(2):
            for h in range(2):
                if d < WIN:
                    @pl.when((s >= d) & (s < lines - 1))
                    def _():
                        back(which, d + 1, h).wait_recv()
                        tmp[which, h] = tmp[which, h] + gin[which, 2 * d + h].astype(F32)
                if d > 0:
                    @pl.when(s >= d)
                    def _():
                        gout[which, 2 * d + h] = tmp[which, h].astype(BF16)
                        back(which, d, h).start()

    for which, (dst, recv) in enumerate(((dksend, dkrecv), (dvsend, dvrecv))):
        for i in range(KV):
            dst[i] = tmp[which, i // 4, (i % 4) * TOK:(i % 4 + 1) * TOK, :].astype(BF16)
        for p in range(1, KV):
            peer = lax.rem(j + p, KV)
            line_copy(2 + which, dst.at[peer], recv.at[j], peer, j, (out_s, out_r)).start()
        recv[j] = dst[j]

    def returned(kind, peer):
        src = (osend, dqsend, dksend, dvsend)[kind]
        dst = (orecv, dqrecv, dkrecv, dvrecv)[kind]
        line_copy(kind, src.at[peer], dst.at[j], peer, peer, (out_s, out_r)).wait_recv()

    for kind in range(2):
        for p in range(1, KV):
            returned(kind, lax.rem(j + p, KV))
    for pair in range(KV // 2):
        heads = slice(pair * 16, (pair + 1) * 16)
        o = [orecv[2 * pair + u].astype(F32).reshape(TOK, GRP, DH) for u in range(2)]
        o_out[:, heads, :] = jnp.concatenate(o, axis=1).astype(BF16)
        x = [rope_back(dqrecv[2 * pair + u].astype(F32).reshape(TOK, GRP, DH)) for u in range(2)]
        dq_out[:, heads, :] = jnp.concatenate(x, axis=1).astype(BF16)
    for kind in range(2, 4):
        for p in range(1, KV):
            returned(kind, lax.rem(j + p, KV))
    for h in range(KV):
        stage[pl.ds(h, TOK, stride=KV), :] = dkrecv[h].astype(F32)
    dk_out[...] = rope_back(stage[...].reshape(TOK, KV, DH)).astype(BF16)
    for h in range(KV):
        stage[pl.ds(h, TOK, stride=KV), :] = dvrecv[h].astype(F32)
    dv_out[...] = stage[...].reshape(TOK, KV, DH).astype(BF16)

    for p in range(1, KV):
        peer = lax.rem(j + p, KV)
        for kind, (src, dst) in enumerate(
            ((ksend, own_rows(kwin)), (vsend, own_rows(vwin)), (qsend, qbuf.at[j]), (gsend, gbuf.at[j]))
        ):
            line_copy(kind, src.at[peer], dst, peer, j, (in_s, in_r)).wait_send()
        for kind, (src, dst) in enumerate(
            ((osend, orecv), (dqsend, dqrecv), (dksend, dkrecv), (dvsend, dvrecv))
        ):
            line_copy(kind, src.at[peer], dst.at[j], peer, j, (out_s, out_r)).wait_send()
    for d in range(1, WIN + 1):
        for which in range(2):
            for h in range(2):
                @pl.when((s >= d - 1) & (s < lines - 1))
                def _():
                    hop(which, d, h).wait_send()

                @pl.when(s >= d)
                def _():
                    back(which, d, h).wait_send()


def rope_tables(positions):
    half = DH // 2
    exponent = jnp.arange(half, dtype=F32) * (2.0 / DH)
    frequency = jnp.power(jnp.float32(ROPE_BASE), -exponent)
    angle = positions.astype(F32)[:, None] * frequency[None, :]
    cosine, sine = jnp.cos(angle), jnp.sin(angle)
    return jnp.concatenate([cosine, cosine], axis=1), jnp.concatenate([-sine, sine], axis=1)


def body(lines, q_heads, k_heads, v_heads, d_out, positions, subtree_end, ancestors):
    cosine, sine = rope_tables(positions)
    ends = subtree_end.reshape(-1, BLK)
    vmem = pl.BlockSpec(memory_space=pltpu.VMEM)
    smem = pl.BlockSpec(memory_space=pltpu.SMEM)
    slab = pltpu.VMEM((KV, TOK, DH), BF16)
    rows = pltpu.VMEM((KV, ROWS, DH), BF16)
    window = pltpu.VMEM((2 * WIN + 2, BLK, DH), BF16)
    dma = pltpu.SemaphoreType.DMA
    return pl.pallas_call(
        functools.partial(kernel, lines),
        out_shape=(
            jax.ShapeDtypeStruct(q_heads.shape, BF16),
            jax.ShapeDtypeStruct(q_heads.shape, BF16),
            jax.ShapeDtypeStruct(k_heads.shape, BF16),
            jax.ShapeDtypeStruct(v_heads.shape, BF16),
        ),
        in_specs=[vmem] * 6 + [smem, vmem],
        out_specs=(vmem,) * 4,
        scratch_shapes=[
            pltpu.VMEM((ROWS, DH), F32),
            slab, slab,
            rows, rows, rows, rows,
            window, window,
            pltpu.VMEM((2, KEYS, DH), BF16),
            pltpu.VMEM((2, KEYS, DH), BF16),
            pltpu.VMEM((2, DH, KEYS), BF16),
            pltpu.VMEM((2, DH, KEYS), BF16),
            pltpu.VMEM((KV, KEYS, ROWS), F32),
            pltpu.VMEM((8, 128), F32),
            pltpu.VMEM((16, 128), BF16),
            pltpu.VMEM((2 * ANC + 1, BLK, DH), F32),
            pltpu.VMEM((2 * ANC + 1, BLK, DH), F32),
            rows, rows, rows, rows,
            pltpu.VMEM((2, 2, BLK, DH), F32),
            pltpu.VMEM((2, 2 * WIN + 2, BLK, DH), BF16),
            pltpu.VMEM((2, 2 * WIN, BLK, DH), BF16),
            slab, slab, slab, slab,
            dma((4, KV)), dma((4, KV)),
            dma((4, WIN + 1)), dma((4, WIN + 1)),
            dma((4, WIN + 1)), dma((4, WIN + 1)),
            dma((4, KV)), dma((4, KV)),
        ],
        compiler_params=pltpu.CompilerParams(
            collective_id=0, has_side_effects=True, vmem_limit_bytes=56 << 20
        ),
        cost_estimate=pl.CostEstimate(
            flops=2 * 5 * KV * KEYS * ROWS * DH, bytes_accessed=4 << 20, transcendentals=KV * KEYS * ROWS
        ),
    )(q_heads, k_heads, v_heads, d_out, cosine, sine, ancestors, ends)


def solution(mesh):
    token = P(("seq", "kv"), None, None)
    return jax.shard_map(
        functools.partial(body, mesh.shape["seq"]),
        mesh=mesh,
        in_specs=(token, token, token, token, P(("seq", "kv")), P(), P("seq", None)),
        out_specs=(token, token, token, token),
        check_vma=False,
    )
```

```python
import functools
import math

import jax
import jax.numpy as jnp
import numpy as np
from jax import lax
from jax.experimental import pallas as pl
from jax.experimental.pallas import tpu as pltpu
from jax.sharding import PartitionSpec as P

MESH = pl.DeviceIdType.MESH
BF16, F32 = jnp.bfloat16, jnp.float32
BLK = 128
ANC = 6
WIN = 7
KV = 8
GRP = 8
TOK = 32
DH = 128
ROWS = TOK * GRP
KEYS = ANC * BLK
ROPE_BASE = 500000.0
HIDDEN = -1e30
SCALE = 1.0 / math.sqrt(DH)
LOG2E = 1.4426950408889634
NT = (((1,), (1,)), ((), ()))
NN = (((1,), (0,)), ((), ()))


def dot(a, b, dims=NN):
    return lax.dot_general(a, b, dims, preferred_element_type=F32)


def kernel(
    lines,
    q_ref, k_ref, v_ref, g_ref, pos_ref, freq_ref, anc_ref, end_ref,
    o_out, dq_out, dk_out, dv_out,
    cos_ref, sin_ref, stage, ksend, vsend, qsend, gsend, qbuf, gbuf, kwin, vwin,
    kb, vb, kbt, vbt, bias, prob, plow, dka, dva,
    osend, dqsend, orecv, dqrecv, tmp, gout, gin, dsend, drecv, ofin, dqfin, dkfin, dvfin,
    line_s, line_r, next_s, next_r, win_s, win_r, grad_s, grad_r, fin,
):
    s = lax.axis_index("seq")
    j = lax.axis_index("kv")
    left, right = s - 1, s + 1
    has_left, has_right = s > 0, s < lines - 1

    barrier = pltpu.get_barrier_semaphore()

    def greet(line, peer):
        pl.semaphore_signal(barrier, inc=1, device_id=(line, peer), device_id_type=MESH)

    for p in range(1, KV):
        greet(s, lax.rem(j + p, KV))

    @pl.when(has_left)
    def _():
        for p in range(KV):
            greet(left, lax.rem(j + p, KV))

    @pl.when(has_right)
    def _():
        for p in range(KV):
            greet(right, lax.rem(j + p, KV))

    stage[...] = v_ref[...].astype(F32).reshape(ROWS, DH)
    for h in range(KV):
        vsend[h] = stage[pl.ds(h, TOK, stride=KV), :].astype(BF16)

    across = jnp.broadcast_to(pos_ref[...].astype(F32), (TOK, TOK))
    row = lax.broadcasted_iota(jnp.int32, (TOK, TOK), 0)
    lane = lax.broadcasted_iota(jnp.int32, (TOK, TOK), 1)
    position = jnp.sum(jnp.where(row == lane, across, 0.0), axis=1, keepdims=True)
    angle = position * freq_ref[...]
    lane = lax.broadcasted_iota(jnp.int32, (TOK, DH), 1)
    cos_ref[...] = jnp.cos(angle)
    sin_ref[...] = jnp.where(lane < DH // 2, -1.0, 1.0) * jnp.sin(angle)

    def rope(x):
        return x * cos_ref[...][:, None, :] + pltpu.roll(x, DH // 2, 2) * sin_ref[...][:, None, :]

    def rope_back(x):
        return x * cos_ref[...][:, None, :] - pltpu.roll(x, DH // 2, 2) * sin_ref[...][:, None, :]

    stage[...] = rope(k_ref[...].astype(F32)).reshape(ROWS, DH)
    for h in range(KV):
        ksend[h] = stage[pl.ds(h, TOK, stride=KV), :].astype(BF16)

    pl.semaphore_wait(
        barrier, KV - 1 + KV * has_left.astype(jnp.int32) + KV * has_right.astype(jnp.int32)
    )

    def line_copy(kind, src, dst, peer, slot):
        return pltpu.make_async_remote_copy(
            src_ref=src, dst_ref=dst, send_sem=line_s.at[kind, peer],
            recv_sem=line_r.at[kind, slot], device_id=(s, peer), device_id_type=MESH,
        )

    def next_copy(kind, src, dst, line, peer, slot):
        return pltpu.make_async_remote_copy(
            src_ref=src, dst_ref=dst, send_sem=next_s.at[kind, peer],
            recv_sem=next_r.at[kind, slot], device_id=(line, peer), device_id_type=MESH,
        )

    mine = pl.ds(pl.multiple_of(lax.rem(j, 4) * TOK, TOK), TOK)

    slabs, wins = (ksend, vsend), (kwin, vwin)

    def kv_here(which, peer, slot):
        return line_copy(which, slabs[which].at[peer], wins[which].at[j // 4, mine], peer, slot)

    def kv_next(which, peer, slot):
        return next_copy(which, slabs[which].at[peer], wins[which].at[2 + j // 4, mine], right, peer, slot)

    @pl.when(has_right)
    def _():
        for which in range(2):
            for p in range(KV):
                peer = lax.rem(j + p, KV)
                kv_next(which, peer, j).start()

    for which in range(2):
        for p in range(1, KV):
            peer = lax.rem(j + p, KV)
            kv_here(which, peer, j).start()
        wins[which][j // 4, mine, :] = slabs[which][j]

    for pair in range(KV // 2):
        x = q_ref[:, pair * 16:(pair + 1) * 16, :].astype(F32).reshape(TOK, 2, GRP, DH)
        y = g_ref[:, pair * 16:(pair + 1) * 16, :].astype(F32).reshape(TOK, 2, GRP, DH)
        for u in range(2):
            qsend[2 * pair + u] = rope(x[:, u]).reshape(ROWS, DH).astype(BF16)
            gsend[2 * pair + u] = y[:, u].reshape(ROWS, DH).astype(BF16)
    for p in range(1, KV):
        peer = lax.rem(j + p, KV)
        line_copy(2, qsend.at[peer], qbuf.at[j], peer, j).start()
        line_copy(3, gsend.at[peer], gbuf.at[j], peer, j).start()
    qbuf[j] = qsend[j]
    gbuf[j] = gsend[j]

    def hop(which, d, h):
        return pltpu.make_async_remote_copy(
            src_ref=wins[which].at[2 * (d - 1) + h], dst_ref=wins[which].at[2 * d + h],
            send_sem=win_s.at[2 * which + h, d], recv_sem=win_r.at[2 * which + h, d],
            device_id=(right, j), device_id_type=MESH,
        )

    for d in range(2, WIN + 1):
        for which in range(2):
            for h in range(2):
                if d > 2:
                    @pl.when(s >= d - 1)
                    def _():
                        hop(which, d - 1, h).wait_recv()
                else:
                    @pl.when(has_left)
                    def _():
                        for r in range(4):
                            kv_next(which, 4 * h + r, 4 * h + r).wait_recv()

                @pl.when((s >= d - 1) & has_right)
                def _():
                    hop(which, d, h).start()
        if d == 2:
            def mask_step(u, carry):
                b = u // ANC
                slot = lax.rem(u, ANC)
                a = anc_ref[b, slot]
                ends = end_ref[pl.ds(jnp.maximum(a, 0), 1), :].astype(F32)
                last = jnp.broadcast_to(ends, (BLK, BLK)).T
                last = jnp.where(a >= 0, last, -1.0)
                first = (a * BLK + lax.broadcasted_iota(jnp.int32, (BLK, BLK), 0)).astype(F32)
                token = lax.broadcasted_iota(jnp.int32, (BLK, BLK), 1) // GRP
                for c in range(4):
                    for half in range(2):
                        query = ((2 * s + b) * BLK + c * TOK + half * (TOK // 2) + token).astype(F32)
                        seen = (query >= first) & (query <= last)
                        bias[4 * b + c, pl.ds(pl.multiple_of(slot * BLK, BLK), BLK),
                             half * BLK:(half + 1) * BLK] = jnp.where(seen, 0.0, HIDDEN)
                return carry

            lax.fori_loop(0, 2 * ANC, mask_step, 0)
            dka[...] = jnp.zeros_like(dka)
            dva[...] = jnp.zeros_like(dva)

    def last_hop(which):
        for h in range(2):
            @pl.when(s >= WIN)
            def _():
                hop(which, WIN, h).wait_recv()

    def gather(which, block, turned):
        def step(u, carry):
            b = u // ANC
            slot = lax.rem(u, ANC)
            a = anc_ref[b, slot]
            index = 2 * (s - lax.shift_right_arithmetic(a, 1)) + (a & 1)
            index = jnp.where(a >= 0, jnp.clip(index, 0, 2 * WIN + 1), 0)
            rows = pl.ds(pl.multiple_of(slot * BLK, BLK), BLK)
            entry = wins[which][index]
            block[b, rows, :] = entry
            turned[b, :, rows] = entry.astype(F32).T.astype(BF16)
            return carry

        lax.fori_loop(0, 2 * ANC, step, 0)

    for p in range(1, KV):
        peer = lax.rem(j + p, KV)
        kv_here(0, peer, peer).wait_recv()
        kv_here(1, peer, peer).wait_recv()
    last_hop(0)
    gather(0, kb, kbt)
    for p in range(1, KV):
        peer = lax.rem(j + p, KV)
        line_copy(2, qsend.at[peer], qbuf.at[j], peer, peer).wait_recv()
        line_copy(3, gsend.at[peer], gbuf.at[j], peer, peer).wait_recv()

    def forward(p, carry):
        i = lax.rem(j + p, KV)
        b = i // 4
        scores = dot(kb[b], qbuf[i], NT) * (SCALE * LOG2E) + bias[i]
        top = jnp.max(scores, axis=0, keepdims=True)
        weight = jnp.exp2(scores - top)
        weight = weight * (1.0 / jnp.sum(weight, axis=0, keepdims=True))
        prob[i] = weight
        low = weight.astype(BF16)
        plow[i] = low
        dva[pl.ds(b * ANC, ANC)] += dot(low, gbuf[i]).reshape(ANC, BLK, DH)
        return carry

    lax.fori_loop(1, KV + 1, forward, 0)

    def back(which, d, h):
        return pltpu.make_async_remote_copy(
            src_ref=gout.at[which, 2 * d + h], dst_ref=gin.at[which, 2 * (d - 1) + h],
            send_sem=grad_s.at[2 * which + h, d], recv_sem=grad_r.at[2 * which + h, d - 1],
            device_id=(left, j), device_id_type=MESH,
        )

    def place(b, block):
        index = 2 * ANC
        for slot in range(ANC):
            hit = (anc_ref[b, slot] == block) & (block >= 0)
            index = jnp.where(hit, b * ANC + slot, index)
        return index

    def grad_step(which, d):
        acc = (dka, dva)[which]
        for h in range(2):
            block = 2 * (s - d) + h
            tmp[h] = acc[place(0, block)] + acc[place(1, block)]
            if 0 < d < WIN:
                @pl.when((s >= d) & has_right)
                def _():
                    back(which, d + 1, h).wait_recv()
                    tmp[h] = tmp[h] + gin[which, 2 * d + h].astype(F32)
            if d > 1:
                @pl.when(s >= d)
                def _():
                    gout[which, 2 * d + h] = tmp[h].astype(BF16)
                    back(which, d, h).start()
            else:
                for r in range(4):
                    dsend[d, 4 * h + r, which] = tmp[h, r * TOK:(r + 1) * TOK, :].astype(BF16)

    def backward(p, carry):
        i = lax.rem(j + p, KV)
        b = i // 4
        low, cotangent = plow[i], gbuf[i]
        attended = dot(vbt[b], low).astype(BF16)
        osend[i] = attended.astype(F32).T.astype(BF16)
        inner = jnp.sum(cotangent.astype(F32).T * attended.astype(F32), axis=0, keepdims=True)
        dprob = dot(vb[b], cotangent, NT)
        dscore = (prob[i] * (dprob - inner) * SCALE).astype(BF16)
        dka[pl.ds(b * ANC, ANC)] += dot(dscore, qbuf[i]).reshape(ANC, BLK, DH)
        dqsend[i] = dot(kbt[b], dscore).T.astype(BF16)

        @pl.when(i != j)
        def _():
            line_copy(4, osend.at[i], orecv.at[j], i, j).start()
            line_copy(5, dqsend.at[i], dqrecv.at[j], i, j).start()

        @pl.when(i == j)
        def _():
            orecv[j] = osend[i]
            dqrecv[j] = dqsend[i]

        return carry

    def finish(pair):
        for u in range(2):
            peer = 2 * pair + u

            @pl.when(peer != j)
            def _():
                line_copy(4, osend.at[peer], orecv.at[j], peer, peer).wait_recv()
                line_copy(5, dqsend.at[peer], dqrecv.at[j], peer, peer).wait_recv()
        heads = slice(pair * 16, (pair + 1) * 16)
        x = [orecv[2 * pair + u].astype(F32).reshape(TOK, GRP, DH) for u in range(2)]
        ofin[:, heads, :] = jnp.concatenate(x, axis=1).astype(BF16)
        x = [rope_back(dqrecv[2 * pair + u].astype(F32).reshape(TOK, GRP, DH)) for u in range(2)]
        dqfin[:, heads, :] = jnp.concatenate(x, axis=1).astype(BF16)

    grad_step(1, WIN)
    last_hop(1)
    gather(1, vb, vbt)
    lax.fori_loop(1, KV // 2 + 1, backward, 0)
    grad_step(1, WIN - 1)
    lax.fori_loop(KV // 2 + 1, KV + 1, backward, 0)
    grad_step(0, WIN)
    grad_step(1, WIN - 2)
    grad_step(0, 0)
    grad_step(1, 0)

    def d_here(peer, slot):
        return line_copy(6, dsend.at[0, peer], drecv.at[0, j], peer, slot)

    def d_next(peer, slot):
        return next_copy(2, dsend.at[1, peer], drecv.at[1, j], left, peer, slot)

    for p in range(1, KV):
        peer = lax.rem(j + p, KV)
        d_here(peer, j).start()
    drecv[0, j] = dsend[0, j]

    for d in range(WIN - 1, 0, -1):
        grad_step(0, d)
        if d > 2:
            grad_step(1, d - 2)
        if d in (2, 3):
            finish(3 - d)

    @pl.when(has_left)
    def _():
        for p in range(KV):
            peer = lax.rem(j + p, KV)
            d_next(peer, j).start()

    finish(2)
    finish(3)
    done = [pltpu.make_async_copy(ofin, o_out, fin.at[0]), pltpu.make_async_copy(dqfin, dq_out, fin.at[1]),
            pltpu.make_async_copy(dkfin, dk_out, fin.at[2]), pltpu.make_async_copy(dvfin, dv_out, fin.at[3])]
    done[0].start()
    done[1].start()
    for p in range(1, KV):
        peer = lax.rem(j + p, KV)
        d_here(peer, peer).wait_recv()

    @pl.when(has_right)
    def _():
        for p in range(KV):
            d_next(p, p).wait_recv()

    @pl.when(jnp.logical_not(has_right))
    def _():
        drecv[1] = jnp.zeros_like(drecv[1])

    for which in range(2):
        for h in range(KV):
            total = drecv[0, h, which].astype(F32) + drecv[1, h, which].astype(F32)
            stage[pl.ds(h, TOK, stride=KV), :] = total
        total = stage[...].reshape(TOK, KV, DH).astype(BF16)
        if which == 0:
            dkfin[...] = rope_back(total.astype(F32)).astype(BF16)
        else:
            dvfin[...] = total
        done[2 + which].start()

    for p in range(1, KV):
        peer = lax.rem(j + p, KV)
        kv_here(0, peer, j).wait_send()
        kv_here(1, peer, j).wait_send()
        line_copy(2, qsend.at[peer], qbuf.at[j], peer, j).wait_send()
        line_copy(3, gsend.at[peer], gbuf.at[j], peer, j).wait_send()
        line_copy(4, osend.at[peer], orecv.at[j], peer, j).wait_send()
        line_copy(5, dqsend.at[peer], dqrecv.at[j], peer, j).wait_send()
        d_here(peer, j).wait_send()

    @pl.when(has_right)
    def _():
        for p in range(KV):
            kv_next(0, p, j).wait_send()
            kv_next(1, p, j).wait_send()

    @pl.when(has_left)
    def _():
        for p in range(KV):
            d_next(p, j).wait_send()

    for d in range(2, WIN + 1):
        for which in range(2):
            for h in range(2):
                @pl.when((s >= d - 1) & has_right)
                def _():
                    hop(which, d, h).wait_send()

                @pl.when(s >= d)
                def _():
                    back(which, d, h).wait_send()
    for copy in done:
        copy.wait()


def copy_kernel(a, b, c, d, e, f, g, h, sems):
    copies = [pltpu.make_async_copy(x, y, sems.at[n]) for n, (x, y) in enumerate(((a, e), (b, f), (c, g), (d, h)))]
    for copy in copies:
        copy.start()
    for copy in copies:
        copy.wait()


def body(lines, q_heads, k_heads, v_heads, d_out, positions, subtree_end, ancestors):
    frequency = ROPE_BASE ** (-2.0 * (np.arange(DH) % (DH // 2)) / DH)
    frequency = jnp.asarray(frequency[None, :], F32)
    vmem = pl.BlockSpec(memory_space=pltpu.VMEM)
    smem = pl.BlockSpec(memory_space=pltpu.SMEM)
    hbm = pl.BlockSpec(memory_space=pl.ANY)
    rows = pltpu.VMEM((KV, ROWS, DH), BF16)
    dma = pltpu.SemaphoreType.DMA
    shapes = tuple(jax.ShapeDtypeStruct(x.shape, BF16) for x in (q_heads, q_heads, k_heads, v_heads))
    outs = pl.pallas_call(
        functools.partial(kernel, lines),
        out_shape=shapes,
        in_specs=[vmem] * 6 + [smem, vmem],
        out_specs=(hbm,) * 4,
        scratch_shapes=[
            pltpu.VMEM((TOK, DH), F32),
            pltpu.VMEM((TOK, DH), F32),
            pltpu.VMEM((ROWS, DH), F32),
            pltpu.VMEM((KV, TOK, DH), BF16),
            pltpu.VMEM((KV, TOK, DH), BF16),
            rows, rows, rows, rows,
            pltpu.VMEM((2 * WIN + 2, BLK, DH), BF16),
            pltpu.VMEM((2 * WIN + 2, BLK, DH), BF16),
            pltpu.VMEM((2, KEYS, DH), BF16),
            pltpu.VMEM((2, KEYS, DH), BF16),
            pltpu.VMEM((2, DH, KEYS), BF16),
            pltpu.VMEM((2, DH, KEYS), BF16),
            pltpu.VMEM((KV, KEYS, ROWS), F32),
            pltpu.VMEM((KV, KEYS, ROWS), F32),
            pltpu.VMEM((KV, KEYS, ROWS), BF16),
            pltpu.VMEM((2 * ANC + 1, BLK, DH), F32),
            pltpu.VMEM((2 * ANC + 1, BLK, DH), F32),
            rows, rows, rows, rows,
            pltpu.VMEM((2, BLK, DH), F32),
            pltpu.VMEM((2, 2 * WIN + 2, BLK, DH), BF16),
            pltpu.VMEM((2, 2 * WIN, BLK, DH), BF16),
            pltpu.VMEM((2, KV, 2, TOK, DH), BF16),
            pltpu.VMEM((2, KV, 2, TOK, DH), BF16),
            pltpu.VMEM(q_heads.shape, BF16),
            pltpu.VMEM(q_heads.shape, BF16),
            pltpu.VMEM(k_heads.shape, BF16),
            pltpu.VMEM(k_heads.shape, BF16),
            dma((7, KV)), dma((7, KV)),
            dma((3, KV)), dma((3, KV)),
            dma((4, WIN + 1)), dma((4, WIN + 1)),
            dma((4, WIN + 1)), dma((4, WIN + 1)),
            dma((4,)),
        ],
        compiler_params=pltpu.CompilerParams(
            collective_id=0, has_side_effects=True, vmem_limit_bytes=56 << 20
        ),
        cost_estimate=pl.CostEstimate(
            flops=2 * 5 * KV * KEYS * ROWS * DH, bytes_accessed=4 << 20, transcendentals=KV * KEYS * ROWS
        ),
    )(q_heads, k_heads, v_heads, d_out, positions.reshape(1, TOK), frequency, ancestors, subtree_end.reshape(-1, BLK))
    return pl.pallas_call(
        copy_kernel,
        out_shape=shapes,
        in_specs=[vmem] * 4,
        out_specs=(hbm,) * 4,
        scratch_shapes=[dma((4,))],
    )(*outs)


def solution(mesh):
    token = P(("seq", "kv"), None, None)
    return jax.shard_map(
        functools.partial(body, mesh.shape["seq"]),
        mesh=mesh,
        in_specs=(token, token, token, token, P(("seq", "kv")), P(), P("seq", None)),
        out_specs=(token, token, token, token),
        check_vma=False,
    )
```

```python
import functools
import math

import jax
import jax.numpy as jnp
import numpy as np
from jax import lax
from jax.experimental import pallas as pl
from jax.experimental.pallas import tpu as pltpu
from jax.sharding import PartitionSpec as P

MESH = pl.DeviceIdType.MESH
BF16, F32 = jnp.bfloat16, jnp.float32
BLK = 128
ANC = 6
WIN = 7
KV = 8
GRP = 8
TOK = 32
DH = 128
ROWS = TOK * GRP
KEYS = ANC * BLK
ROPE_BASE = 500000.0
HIDDEN = -1e30
SCALE = 1.0 / math.sqrt(DH)
LOG2E = 1.4426950408889634
NT = (((1,), (1,)), ((), ()))
NN = (((1,), (0,)), ((), ()))


def dot(a, b, dims=NN):
    return lax.dot_general(a, b, dims, preferred_element_type=F32)


def kernel(
    lines,
    q_in, k_in, v_in, g_in, pos_in, freq_in, anc_in, end_in,
    o_out, dq_out, dk_out, dv_out,
    q_ref, k_ref, v_ref, g_ref, pos_ref, freq_ref, anc_ref, end_ref, cos_ref, sin_ref, stage, ksend, vsend, qsend, gsend, qbuf, gbuf, kwin, vwin,
    kb, vb, kbt, vbt, bias, prob, plow, work, dlow, norm, dka, dva,
    osend, dqsend, orecv, dqrecv, tmp, gout, gin, dsend, drecv, ofin, dqfin, dkfin, dvfin,
    line_s, line_r, next_s, next_r, win_s, win_r, grad_s, grad_r, fin, load,
):
    s = lax.axis_index("seq")
    j = lax.axis_index("kv")
    left, right = s - 1, s + 1
    has_left, has_right = s > 0, s < lines - 1

    loads = [
        pltpu.make_async_copy(src, dst, load.at[n])
        for n, (src, dst) in enumerate((
            (v_in, v_ref), (pos_in, pos_ref), (freq_in, freq_ref), (k_in, k_ref),
            (q_in, q_ref), (g_in, g_ref), (end_in, end_ref), (anc_in, anc_ref),
        ))
    ]
    for copy in loads:
        copy.start()

    barrier = pltpu.get_barrier_semaphore()

    def greet(line, peer):
        pl.semaphore_signal(barrier, inc=1, device_id=(line, peer), device_id_type=MESH)

    for p in range(1, KV):
        greet(s, lax.rem(j + p, KV))

    @pl.when(has_left)
    def _():
        for p in range(KV):
            greet(left, lax.rem(j + p, KV))

    @pl.when(has_right)
    def _():
        for p in range(KV):
            greet(right, lax.rem(j + p, KV))

    for copy in loads[:4]:
        copy.wait()
    stage[...] = v_ref[...].astype(F32).reshape(ROWS, DH)
    for h in range(KV):
        vsend[h] = stage[pl.ds(h, TOK, stride=KV), :].astype(BF16)

    across = jnp.broadcast_to(pos_ref[...].astype(F32), (TOK, TOK))
    row = lax.broadcasted_iota(jnp.int32, (TOK, TOK), 0)
    lane = lax.broadcasted_iota(jnp.int32, (TOK, TOK), 1)
    position = jnp.sum(jnp.where(row == lane, across, 0.0), axis=1, keepdims=True)
    angle = position * freq_ref[...]
    lane = lax.broadcasted_iota(jnp.int32, (TOK, DH), 1)
    cos_ref[...] = jnp.cos(angle)
    sin_ref[...] = jnp.where(lane < DH // 2, -1.0, 1.0) * jnp.sin(angle)

    def rope(x):
        return x * cos_ref[...][:, None, :] + pltpu.roll(x, DH // 2, 2) * sin_ref[...][:, None, :]

    def rope_back(x):
        return x * cos_ref[...][:, None, :] - pltpu.roll(x, DH // 2, 2) * sin_ref[...][:, None, :]

    stage[...] = rope(k_ref[...].astype(F32)).reshape(ROWS, DH)
    for h in range(KV):
        ksend[h] = stage[pl.ds(h, TOK, stride=KV), :].astype(BF16)

    for copy in loads[4:]:
        copy.wait()

    for pair in range(KV // 2):
        x = q_ref[:, pair * 16:(pair + 1) * 16, :].astype(F32).reshape(TOK, 2, GRP, DH)
        y = g_ref[:, pair * 16:(pair + 1) * 16, :].astype(F32).reshape(TOK, 2, GRP, DH)
        for u in range(2):
            qsend[2 * pair + u] = rope(x[:, u]).reshape(ROWS, DH).astype(BF16)
            gsend[2 * pair + u] = y[:, u].reshape(ROWS, DH).astype(BF16)

    pl.semaphore_wait(
        barrier, KV - 1 + KV * has_left.astype(jnp.int32) + KV * has_right.astype(jnp.int32)
    )

    def line_copy(kind, src, dst, peer):
        return pltpu.make_async_remote_copy(
            src_ref=src, dst_ref=dst, send_sem=line_s.at[kind],
            recv_sem=line_r.at[kind], device_id=(s, peer), device_id_type=MESH,
        )

    def next_copy(kind, slot, src, dst, line, peer):
        return pltpu.make_async_remote_copy(
            src_ref=src, dst_ref=dst, send_sem=next_s.at[kind],
            recv_sem=next_r.at[slot], device_id=(line, peer), device_id_type=MESH,
        )

    others = pl.ds(0, KV - 1)

    mine = pl.ds(pl.multiple_of(lax.rem(j, 4) * TOK, TOK), TOK)

    slabs, wins = (ksend, vsend), (kwin, vwin)

    def kv_here(which, peer):
        return line_copy(which, slabs[which].at[peer], wins[which].at[j // 4, mine], peer)

    def kv_next(which, peer):
        return next_copy(
            which, 2 * which + j // 4, slabs[which].at[peer], wins[which].at[2 + j // 4, mine], right, peer
        )

    @pl.when(has_right)
    def _():
        for which in range(2):
            for p in range(KV):
                peer = lax.rem(j + p, KV)
                kv_next(which, peer).start()

    for which in range(2):
        for p in range(1, KV):
            peer = lax.rem(j + p, KV)
            kv_here(which, peer).start()
        wins[which][j // 4, mine, :] = slabs[which][j]

    for p in range(1, KV):
        peer = lax.rem(j + p, KV)
        line_copy(2, qsend.at[peer], qbuf.at[j], peer).start()
        line_copy(3, gsend.at[peer], gbuf.at[j], peer).start()
    qbuf[j] = qsend[j]
    gbuf[j] = gsend[j]

    def hop(which, d, h):
        return pltpu.make_async_remote_copy(
            src_ref=wins[which].at[2 * (d - 1) + h], dst_ref=wins[which].at[2 * d + h],
            send_sem=win_s.at[which], recv_sem=win_r.at[2 * which + h, d - 2],
            device_id=(right, j), device_id_type=MESH,
        )

    for d in range(2, WIN + 1):
        for which in range(2):
            for h in range(2):
                if d > 2:
                    @pl.when(s >= d - 1)
                    def _():
                        hop(which, d - 1, h).wait_recv()
                else:
                    @pl.when(has_left)
                    def _():
                        half = wins[which].at[2 + h]
                        next_copy(which, 2 * which + h, half, half, right, j).wait_recv()

                @pl.when((s >= d - 1) & has_right)
                def _():
                    hop(which, d, h).start()
        if d == 2:
            def mask_step(u, carry):
                b = u // ANC
                slot = lax.rem(u, ANC)
                a = anc_ref[b, slot]
                ends = end_ref[pl.ds(jnp.maximum(a, 0), 1), :].astype(F32)
                last = jnp.broadcast_to(ends, (BLK, BLK)).T
                last = jnp.where(a >= 0, last, -1.0)
                first = (a * BLK + lax.broadcasted_iota(jnp.int32, (BLK, BLK), 0)).astype(F32)
                token = lax.broadcasted_iota(jnp.int32, (BLK, BLK), 1) // GRP
                for c in range(4):
                    for half in range(2):
                        query = ((2 * s + b) * BLK + c * TOK + half * (TOK // 2) + token).astype(F32)
                        seen = (query >= first) & (query <= last)
                        bias[4 * b + c, pl.ds(pl.multiple_of(slot * BLK, BLK), BLK),
                             half * BLK:(half + 1) * BLK] = jnp.where(seen, 0.0, HIDDEN)
                return carry

            lax.fori_loop(0, 2 * ANC, mask_step, 0)
            dka[...] = jnp.zeros_like(dka)
            dva[...] = jnp.zeros_like(dva)

    def last_hop(which):
        for h in range(2):
            @pl.when(s >= WIN)
            def _():
                hop(which, WIN, h).wait_recv()

    def gather(which, block, turned):
        def step(u, carry):
            b = u // ANC
            slot = lax.rem(u, ANC)
            a = anc_ref[b, slot]
            index = 2 * (s - lax.shift_right_arithmetic(a, 1)) + (a & 1)
            index = jnp.where(a >= 0, jnp.clip(index, 0, 2 * WIN + 1), 0)
            rows = pl.ds(pl.multiple_of(slot * BLK, BLK), BLK)
            entry = wins[which][index]
            block[b, rows, :] = entry
            turned[b, :, rows] = entry.astype(F32).T.astype(BF16)
            return carry

        lax.fori_loop(0, 2 * ANC, step, 0)

    for which in range(2):
        line_copy(which, slabs[which].at[others], slabs[which].at[others], j).wait_recv()
    last_hop(0)
    gather(0, kb, kbt)
    line_copy(2, qsend.at[others], qbuf.at[others], j).wait_recv()
    line_copy(3, gsend.at[others], gbuf.at[others], j).wait_recv()

    def forward(p, carry):
        i = lax.rem(j + p, KV)
        b = i // 4
        slots = [slice(n * BLK, (n + 1) * BLK) for n in range(ANC)]
        work[...] = dot(kb[b], qbuf[i], NT)

        def score(n):
            return work[slots[n], :] * (SCALE * LOG2E) + bias[i, slots[n], :]

        top = jnp.max(score(0), axis=0, keepdims=True)
        for n in range(1, ANC):
            top = jnp.maximum(top, jnp.max(score(n), axis=0, keepdims=True))
        total = jnp.zeros((1, ROWS), F32)
        for n in range(ANC):
            weight = jnp.exp2(score(n) - top)
            prob[i, slots[n], :] = weight
            total = total + jnp.sum(weight, axis=0, keepdims=True)
        share = 1.0 / total
        norm[i] = share
        for n in range(ANC):
            plow[i, slots[n], :] = (prob[i, slots[n], :] * share).astype(BF16)
        dva[pl.ds(b * ANC, ANC)] += dot(plow[i], gbuf[i]).reshape(ANC, BLK, DH)
        return carry

    lax.fori_loop(1, KV + 1, forward, 0)

    def back(which, d, h):
        return pltpu.make_async_remote_copy(
            src_ref=gout.at[which, 2 * d + h], dst_ref=gin.at[which, 2 * (d - 1) + h],
            send_sem=grad_s.at[which], recv_sem=grad_r.at[2 * which + h, d - 2],
            device_id=(left, j), device_id_type=MESH,
        )

    def place(b, block):
        index = 2 * ANC
        for slot in range(ANC):
            hit = (anc_ref[b, slot] == block) & (block >= 0)
            index = jnp.where(hit, b * ANC + slot, index)
        return index

    def grad_step(which, d):
        acc = (dka, dva)[which]
        for h in range(2):
            block = 2 * (s - d) + h
            tmp[h] = acc[place(0, block)] + acc[place(1, block)]
            if 0 < d < WIN:
                @pl.when((s >= d) & has_right)
                def _():
                    back(which, d + 1, h).wait_recv()
                    tmp[h] = tmp[h] + gin[which, 2 * d + h].astype(F32)
            if d > 1:
                @pl.when(s >= d)
                def _():
                    gout[which, 2 * d + h] = tmp[h].astype(BF16)
                    back(which, d, h).start()
            else:
                for r in range(4):
                    dsend[d, 4 * h + r, which] = tmp[h, r * TOK:(r + 1) * TOK, :].astype(BF16)

    def backward(p, carry):
        i = lax.rem(j + p, KV)
        b = i // 4
        low, cotangent = plow[i], gbuf[i]
        attended = dot(vbt[b], low).astype(BF16)
        osend[i] = attended.astype(F32).T.astype(BF16)
        inner = jnp.sum(cotangent.astype(F32).T * attended.astype(F32), axis=0, keepdims=True)
        work[...] = dot(vb[b], cotangent, NT)
        factor = norm[i] * SCALE
        for n in range(ANC):
            rows = slice(n * BLK, (n + 1) * BLK)
            dlow[rows, :] = (prob[i, rows, :] * ((work[rows, :] - inner) * factor)).astype(BF16)
        dka[pl.ds(b * ANC, ANC)] += dot(dlow[...], qbuf[i]).reshape(ANC, BLK, DH)
        dqsend[i] = dot(kbt[b], dlow[...]).T.astype(BF16)

        @pl.when(i != j)
        def _():
            line_copy(4, osend.at[i], orecv.at[j], i).start()
            line_copy(5, dqsend.at[i], dqrecv.at[j], i).start()

        @pl.when(i == j)
        def _():
            orecv[j] = osend[i]
            dqrecv[j] = dqsend[i]

        return carry

    def finish(pair):
        if pair == 0:
            line_copy(4, osend.at[others], orecv.at[others], j).wait_recv()
            line_copy(5, dqsend.at[others], dqrecv.at[others], j).wait_recv()
        heads = slice(pair * 16, (pair + 1) * 16)
        x = [orecv[2 * pair + u].astype(F32).reshape(TOK, GRP, DH) for u in range(2)]
        ofin[:, heads, :] = jnp.concatenate(x, axis=1).astype(BF16)
        x = [rope_back(dqrecv[2 * pair + u].astype(F32).reshape(TOK, GRP, DH)) for u in range(2)]
        dqfin[:, heads, :] = jnp.concatenate(x, axis=1).astype(BF16)

    grad_step(1, WIN)
    last_hop(1)
    gather(1, vb, vbt)
    lax.fori_loop(1, KV // 2 + 1, backward, 0)
    grad_step(1, WIN - 1)
    lax.fori_loop(KV // 2 + 1, KV + 1, backward, 0)
    grad_step(0, WIN)
    grad_step(1, WIN - 2)
    grad_step(0, 0)
    grad_step(1, 0)

    for p in range(1, KV):
        peer = lax.rem(j + p, KV)
        line_copy(6, dsend.at[0, peer], drecv.at[0, j], peer).start()
    drecv[0, j] = dsend[0, j]

    for d in range(WIN - 1, 0, -1):
        grad_step(0, d)
        if d > 2:
            grad_step(1, d - 2)
        if d in (2, 3):
            finish(3 - d)

    @pl.when(has_left)
    def _():
        for p in range(KV):
            peer = lax.rem(j + p, KV)
            next_copy(2, 4, dsend.at[1, peer], drecv.at[1, j], left, peer).start()

    finish(2)
    finish(3)
    done = [pltpu.make_async_copy(ofin, o_out, fin.at[0]), pltpu.make_async_copy(dqfin, dq_out, fin.at[1]),
            pltpu.make_async_copy(dkfin, dk_out, fin.at[2]), pltpu.make_async_copy(dvfin, dv_out, fin.at[3])]
    done[0].start()
    done[1].start()
    line_copy(6, dsend.at[0, others], drecv.at[0, others], j).wait_recv()

    @pl.when(has_right)
    def _():
        next_copy(2, 4, dsend.at[1], drecv.at[1], right, j).wait_recv()

    @pl.when(jnp.logical_not(has_right))
    def _():
        drecv[1] = jnp.zeros_like(drecv[1])

    for which in range(2):
        for h in range(KV):
            total = drecv[0, h, which].astype(F32) + drecv[1, h, which].astype(F32)
            stage[pl.ds(h, TOK, stride=KV), :] = total
        total = stage[...].reshape(TOK, KV, DH).astype(BF16)
        if which == 0:
            dkfin[...] = rope_back(total.astype(F32)).astype(BF16)
        else:
            dvfin[...] = total
        done[2 + which].start()

    for kind, (src, dst) in enumerate((
        (ksend, ksend), (vsend, vsend), (qsend, qbuf), (gsend, gbuf), (osend, orecv), (dqsend, dqrecv),
        (dsend.at[0], drecv.at[0]),
    )):
        line_copy(kind, src.at[others], dst.at[others], j).wait_send()

    @pl.when(has_right)
    def _():
        for which in range(2):
            next_copy(which, 2 * which, slabs[which], slabs[which], right, j).wait_send()

    @pl.when(has_left)
    def _():
        next_copy(2, 4, dsend.at[1], drecv.at[1], left, j).wait_send()

    for n in range(1, WIN):
        some = pl.ds(0, 2 * n)

        @pl.when((s >= n if n == WIN - 1 else s == n) & has_right)
        def _():
            for which in range(2):
                pltpu.make_async_remote_copy(
                    src_ref=wins[which].at[some], dst_ref=wins[which].at[some], send_sem=win_s.at[which],
                    recv_sem=win_r.at[0, 0], device_id=(right, j), device_id_type=MESH,
                ).wait_send()

        @pl.when(s >= n + 1 if n == WIN - 1 else s == n + 1)
        def _():
            for which in range(2):
                pltpu.make_async_remote_copy(
                    src_ref=gout.at[which, some], dst_ref=gin.at[which, some], send_sem=grad_s.at[which],
                    recv_sem=grad_r.at[0, 0], device_id=(left, j), device_id_type=MESH,
                ).wait_send()
    for copy in done:
        copy.wait()


def copy_kernel(*refs):
    ins, outs, mids, sems = refs[:4], refs[4:8], refs[8:12], refs[12]
    first = [pltpu.make_async_copy(ins[n], mids[n], sems.at[0, n]) for n in range(4)]
    second = [pltpu.make_async_copy(mids[n], outs[n], sems.at[1, n]) for n in range(4)]
    for copy in first:
        copy.start()
    for n in range(4):
        first[n].wait()
        second[n].start()
    for copy in second:
        copy.wait()


def body(lines, q_heads, k_heads, v_heads, d_out, positions, subtree_end, ancestors):
    frequency = ROPE_BASE ** (-2.0 * (np.arange(DH) % (DH // 2)) / DH)
    frequency = jnp.asarray(frequency[None, :], F32)
    hbm = pl.BlockSpec(memory_space=pl.ANY)
    rows = pltpu.VMEM((KV, ROWS, DH), BF16)
    dma = pltpu.SemaphoreType.DMA
    shapes = tuple(jax.ShapeDtypeStruct(x.shape, BF16) for x in (q_heads, q_heads, k_heads, v_heads))
    outs = pl.pallas_call(
        functools.partial(kernel, lines),
        out_shape=shapes,
        in_specs=[hbm] * 8,
        out_specs=(hbm,) * 4,
        scratch_shapes=[
            pltpu.VMEM(q_heads.shape, BF16),
            pltpu.VMEM(k_heads.shape, BF16),
            pltpu.VMEM(k_heads.shape, BF16),
            pltpu.VMEM(q_heads.shape, BF16),
            pltpu.VMEM((1, TOK), jnp.int32),
            pltpu.VMEM((1, DH), F32),
            pltpu.SMEM((2, ANC), jnp.int32),
            pltpu.VMEM((subtree_end.shape[0] // BLK, BLK), jnp.int32),
            pltpu.VMEM((TOK, DH), F32),
            pltpu.VMEM((TOK, DH), F32),
            pltpu.VMEM((ROWS, DH), F32),
            pltpu.VMEM((KV, TOK, DH), BF16),
            pltpu.VMEM((KV, TOK, DH), BF16),
            rows, rows, rows, rows,
            pltpu.VMEM((2 * WIN + 2, BLK, DH), BF16),
            pltpu.VMEM((2 * WIN + 2, BLK, DH), BF16),
            pltpu.VMEM((2, KEYS, DH), BF16),
            pltpu.VMEM((2, KEYS, DH), BF16),
            pltpu.VMEM((2, DH, KEYS), BF16),
            pltpu.VMEM((2, DH, KEYS), BF16),
            pltpu.VMEM((KV, KEYS, ROWS), F32),
            pltpu.VMEM((KV, KEYS, ROWS), F32),
            pltpu.VMEM((KV, KEYS, ROWS), BF16),
            pltpu.VMEM((KEYS, ROWS), F32),
            pltpu.VMEM((KEYS, ROWS), BF16),
            pltpu.VMEM((KV, 1, ROWS), F32),
            pltpu.VMEM((2 * ANC + 1, BLK, DH), F32),
            pltpu.VMEM((2 * ANC + 1, BLK, DH), F32),
            rows, rows, rows, rows,
            pltpu.VMEM((2, BLK, DH), F32),
            pltpu.VMEM((2, 2 * WIN + 2, BLK, DH), BF16),
            pltpu.VMEM((2, 2 * WIN, BLK, DH), BF16),
            pltpu.VMEM((2, KV, 2, TOK, DH), BF16),
            pltpu.VMEM((2, KV, 2, TOK, DH), BF16),
            pltpu.VMEM(q_heads.shape, BF16),
            pltpu.VMEM(q_heads.shape, BF16),
            pltpu.VMEM(k_heads.shape, BF16),
            pltpu.VMEM(k_heads.shape, BF16),
            dma((7,)), dma((7,)),
            dma((3,)), dma((5,)),
            dma((2,)), dma((4, WIN - 1)),
            dma((2,)), dma((4, WIN - 1)),
            dma((4,)), dma((8,)),
        ],
        compiler_params=pltpu.CompilerParams(
            collective_id=0, has_side_effects=True, vmem_limit_bytes=56 << 20
        ),
        cost_estimate=pl.CostEstimate(
            flops=2 * 5 * KV * KEYS * ROWS * DH, bytes_accessed=4 << 20, transcendentals=KV * KEYS * ROWS
        ),
    )(q_heads, k_heads, v_heads, d_out, positions.reshape(1, TOK), frequency, ancestors, subtree_end.reshape(-1, BLK))
    return pl.pallas_call(
        copy_kernel,
        out_shape=shapes,
        in_specs=[hbm] * 4,
        out_specs=(hbm,) * 4,
        scratch_shapes=[pltpu.VMEM(x.shape, BF16) for x in shapes] + [dma((2, 4))],
    )(*outs)


def solution(mesh):
    token = P(("seq", "kv"), None, None)
    return jax.shard_map(
        functools.partial(body, mesh.shape["seq"]),
        mesh=mesh,
        in_specs=(token, token, token, token, P(("seq", "kv")), P(), P("seq", None)),
        out_specs=(token, token, token, token),
        check_vma=False,
    )
```

```python
import functools
import math

import jax
import jax.numpy as jnp
import numpy as np
from jax import lax
from jax.experimental import pallas as pl
from jax.experimental.pallas import tpu as pltpu
from jax.sharding import PartitionSpec as P

MESH = pl.DeviceIdType.MESH
BF16, F32 = jnp.bfloat16, jnp.float32
BLK = 128
ANC = 6
WIN = 7
KV = 8
GRP = 8
TOK = 32
DH = 128
ROWS = TOK * GRP
KEYS = ANC * BLK
ROPE_BASE = 500000.0
HIDDEN = -1e30
SCALE = 1.0 / math.sqrt(DH)
LOG2E = 1.4426950408889634
NT = (((1,), (1,)), ((), ()))
NN = (((1,), (0,)), ((), ()))


def dot(a, b, dims=NN):
    return lax.dot_general(a, b, dims, preferred_element_type=F32)


def kernel(
    lines,
    q_in, k_in, v_in, g_in, pos_in, freq_in, anc_in, end_in,
    o_out, dq_out, dk_out, dv_out,
    q_ref, k_ref, v_ref, g_ref, pos_ref, freq_ref, anc_ref, end_ref, cos_ref, sin_ref, stage, ksend, vsend, qsend, gsend, qbuf, gbuf, kwin, klast, vwin,
    kb, vb, kbt, vbt, bias, prob, plow, work, dlow, norm, dka, dva,
    osend, dqsend, orecv, dqrecv, tmp, gout, gin, dsend, drecv, ofin, dqfin, dkfin, dvfin,
    line_s, line_r, next_s, next_r, win_s, win_r, grad_s, grad_r, fin, load,
):
    s = lax.axis_index("seq")
    j = lax.axis_index("kv")
    left, right = s - 1, s + 1
    has_left, has_right = s > 0, s < lines - 1

    loads = [
        pltpu.make_async_copy(src, dst, load.at[n])
        for n, (src, dst) in enumerate((
            (v_in, v_ref), (pos_in, pos_ref), (freq_in, freq_ref), (k_in, k_ref),
            (q_in, q_ref), (g_in, g_ref), (end_in, end_ref), (anc_in, anc_ref),
        ))
    ]
    for copy in loads:
        copy.start()

    barrier = pltpu.get_barrier_semaphore()

    def greet(line, peer):
        pl.semaphore_signal(barrier, inc=1, device_id=(line, peer), device_id_type=MESH)

    for p in range(1, KV):
        greet(s, lax.rem(j + p, KV))

    @pl.when(has_left)
    def _():
        for p in range(KV):
            greet(left, lax.rem(j + p, KV))

    @pl.when(has_right)
    def _():
        for p in range(KV):
            greet(right, lax.rem(j + p, KV))

    for copy in loads[:4]:
        copy.wait()
    stage[...] = v_ref[...].astype(F32).reshape(ROWS, DH)
    for h in range(KV):
        vsend[h] = stage[pl.ds(h, TOK, stride=KV), :].astype(BF16)

    across = jnp.broadcast_to(pos_ref[...].astype(F32), (TOK, TOK))
    row = lax.broadcasted_iota(jnp.int32, (TOK, TOK), 0)
    lane = lax.broadcasted_iota(jnp.int32, (TOK, TOK), 1)
    position = jnp.sum(jnp.where(row == lane, across, 0.0), axis=1, keepdims=True)
    angle = position * freq_ref[...]
    lane = lax.broadcasted_iota(jnp.int32, (TOK, DH), 1)
    cos_ref[...] = jnp.cos(angle)
    sin_ref[...] = jnp.where(lane < DH // 2, -1.0, 1.0) * jnp.sin(angle)

    def rope(x):
        return x * cos_ref[...][:, None, :] + pltpu.roll(x, DH // 2, 2) * sin_ref[...][:, None, :]

    def rope_back(x):
        return x * cos_ref[...][:, None, :] - pltpu.roll(x, DH // 2, 2) * sin_ref[...][:, None, :]

    stage[...] = rope(k_ref[...].astype(F32)).reshape(ROWS, DH)
    for h in range(KV):
        ksend[h] = stage[pl.ds(h, TOK, stride=KV), :].astype(BF16)

    for copy in loads[4:]:
        copy.wait()

    for pair in range(KV // 2):
        x = q_ref[:, pair * 16:(pair + 1) * 16, :].astype(F32).reshape(TOK, 2, GRP, DH)
        y = g_ref[:, pair * 16:(pair + 1) * 16, :].astype(F32).reshape(TOK, 2, GRP, DH)
        for u in range(2):
            qsend[2 * pair + u] = rope(x[:, u]).reshape(ROWS, DH).astype(BF16)
            gsend[2 * pair + u] = y[:, u].reshape(ROWS, DH).astype(BF16)

    pl.semaphore_wait(
        barrier, KV - 1 + KV * has_left.astype(jnp.int32) + KV * has_right.astype(jnp.int32)
    )

    def line_copy(kind, src, dst, peer):
        return pltpu.make_async_remote_copy(
            src_ref=src, dst_ref=dst, send_sem=line_s.at[kind],
            recv_sem=line_r.at[kind], device_id=(s, peer), device_id_type=MESH,
        )

    def next_copy(kind, slot, src, dst, line, peer):
        return pltpu.make_async_remote_copy(
            src_ref=src, dst_ref=dst, send_sem=next_s.at[kind],
            recv_sem=next_r.at[slot], device_id=(line, peer), device_id_type=MESH,
        )

    others = pl.ds(0, KV - 1)

    mine = pl.ds(pl.multiple_of(lax.rem(j, 4) * TOK, TOK), TOK)

    slabs, wins = (ksend, vsend), (kwin, vwin)

    def kv_here(which, peer):
        return line_copy(which, slabs[which].at[peer], wins[which].at[j // 4, mine], peer)

    def kv_next(which, peer):
        return next_copy(
            which, 2 * which + j // 4, slabs[which].at[peer], wins[which].at[2 + j // 4, mine], right, peer
        )

    @pl.when(has_right)
    def _():
        for which in range(2):
            for p in range(KV):
                peer = lax.rem(j + p, KV)
                kv_next(which, peer).start()

    for which in range(2):
        for p in range(1, KV):
            peer = lax.rem(j + p, KV)
            kv_here(which, peer).start()
        wins[which][j // 4, mine, :] = slabs[which][j]

    for p in range(1, KV):
        peer = lax.rem(j + p, KV)
        line_copy(2, qsend.at[peer], qbuf.at[j], peer).start()
        line_copy(3, gsend.at[peer], gbuf.at[j], peer).start()
    qbuf[j] = qsend[j]
    gbuf[j] = gsend[j]

    def hop(which, d, h):
        dst = klast.at[h] if which == 0 and d == WIN else wins[which].at[2 * d + h]
        return pltpu.make_async_remote_copy(
            src_ref=wins[which].at[2 * (d - 1) + h], dst_ref=dst,
            send_sem=win_s.at[which], recv_sem=win_r.at[2 * which + h, d - 2],
            device_id=(right, j), device_id_type=MESH,
        )

    for d in range(2, WIN + 1):
        for which in range(2):
            for h in range(2):
                if d > 2:
                    @pl.when(s >= d - 1)
                    def _():
                        hop(which, d - 1, h).wait_recv()
                else:
                    @pl.when(has_left)
                    def _():
                        half = wins[which].at[2 + h]
                        next_copy(which, 2 * which + h, half, half, right, j).wait_recv()

                @pl.when((s >= d - 1) & has_right)
                def _():
                    hop(which, d, h).start()
        if d == 2:
            def mask_step(u, carry):
                b = u // ANC
                slot = lax.rem(u, ANC)
                a = anc_ref[b, slot]
                ends = end_ref[pl.ds(jnp.maximum(a, 0), 1), :].astype(F32)
                last = jnp.broadcast_to(ends, (BLK, BLK)).T
                last = jnp.where(a >= 0, last, -1.0)
                first = (a * BLK + lax.broadcasted_iota(jnp.int32, (BLK, BLK), 0)).astype(F32)
                token = lax.broadcasted_iota(jnp.int32, (BLK, BLK), 1) // GRP
                for c in range(4):
                    for half in range(2):
                        query = ((2 * s + b) * BLK + c * TOK + half * (TOK // 2) + token).astype(F32)
                        seen = (query >= first) & (query <= last)
                        bias[4 * b + c, pl.ds(pl.multiple_of(slot * BLK, BLK), BLK),
                             half * BLK:(half + 1) * BLK] = jnp.where(seen, 0.0, HIDDEN)
                return carry

            lax.fori_loop(0, 2 * ANC, mask_step, 0)
            dka[...] = jnp.zeros_like(dka)
            dva[...] = jnp.zeros_like(dva)

    def last_hop(which):
        for h in range(2):
            @pl.when(s >= WIN)
            def _():
                hop(which, WIN, h).wait_recv()

    def window_slot(b, slot):
        a = anc_ref[b, slot]
        index = 2 * (s - lax.shift_right_arithmetic(a, 1)) + (a & 1)
        return jnp.where(a >= 0, jnp.clip(index, 0, 2 * WIN + 1), 0)

    def slot_rows(slot):
        return pl.ds(pl.multiple_of(slot * BLK, BLK), BLK)

    def near_keys(u, carry):
        b, slot = u // (ANC - 2), 2 + lax.rem(u, ANC - 2)
        kb[b, slot_rows(slot), :] = kwin[jnp.minimum(window_slot(b, slot), 2 * WIN - 1)]
        return carry

    def far_keys(u, carry):
        b, slot = u // 2, lax.rem(u, 2)
        index = window_slot(b, slot)
        near = kwin[jnp.minimum(index, 2 * WIN - 1)].astype(F32)
        far = klast[jnp.maximum(index - 2 * WIN, 0)].astype(F32)
        kb[b, slot_rows(slot), :] = jnp.where(index >= 2 * WIN, far, near).astype(BF16)
        return carry

    def values(u, carry):
        b, slot = u // ANC, lax.rem(u, ANC)
        rows = slot_rows(slot)
        entry = vwin[window_slot(b, slot)]
        vb[b, rows, :] = entry
        vbt[b, :, rows] = entry.astype(F32).T.astype(BF16)
        kbt[b, :, rows] = kb[b, rows, :].astype(F32).T.astype(BF16)
        return carry

    def near_scores(p, carry):
        i = lax.rem(j + p, KV)
        prob[i, 2 * BLK:, :] = dot(kb[i // 4, 2 * BLK:, :], qbuf[i], NT)
        return carry

    for which in range(2):
        line_copy(which, slabs[which].at[others], slabs[which].at[others], j).wait_recv()
    line_copy(2, qsend.at[others], qbuf.at[others], j).wait_recv()
    lax.fori_loop(0, 2 * (ANC - 2), near_keys, 0)
    lax.fori_loop(1, KV + 1, near_scores, 0)
    line_copy(3, gsend.at[others], gbuf.at[others], j).wait_recv()
    last_hop(0)
    lax.fori_loop(0, 4, far_keys, 0)

    def forward(p, carry):
        i = lax.rem(j + p, KV)
        b = i // 4
        slots = [slice(n * BLK, (n + 1) * BLK) for n in range(ANC)]
        prob[i, :2 * BLK, :] = dot(kb[b, :2 * BLK, :], qbuf[i], NT)

        def score(n):
            return prob[i, slots[n], :] * (SCALE * LOG2E) + bias[i, slots[n], :]

        top = jnp.max(score(0), axis=0, keepdims=True)
        for n in range(1, ANC):
            top = jnp.maximum(top, jnp.max(score(n), axis=0, keepdims=True))
        total = jnp.zeros((1, ROWS), F32)
        for n in range(ANC):
            weight = jnp.exp2(score(n) - top)
            prob[i, slots[n], :] = weight
            total = total + jnp.sum(weight, axis=0, keepdims=True)
        share = 1.0 / total
        norm[i] = share
        for n in range(ANC):
            plow[i, slots[n], :] = (prob[i, slots[n], :] * share).astype(BF16)
        dva[pl.ds(b * ANC, ANC)] += dot(plow[i], gbuf[i]).reshape(ANC, BLK, DH)
        return carry

    lax.fori_loop(1, KV + 1, forward, 0)

    def back(which, d, h):
        return pltpu.make_async_remote_copy(
            src_ref=gout.at[which, 2 * d + h], dst_ref=gin.at[which, 2 * (d - 1) + h],
            send_sem=grad_s.at[which], recv_sem=grad_r.at[2 * which + h, d - 2],
            device_id=(left, j), device_id_type=MESH,
        )

    def place(b, block):
        index = 2 * ANC
        for slot in range(ANC):
            hit = (anc_ref[b, slot] == block) & (block >= 0)
            index = jnp.where(hit, b * ANC + slot, index)
        return index

    def grad_step(which, d):
        acc = (dka, dva)[which]
        for h in range(2):
            block = 2 * (s - d) + h
            tmp[h] = acc[place(0, block)] + acc[place(1, block)]
            if 0 < d < WIN:
                @pl.when((s >= d) & has_right)
                def _():
                    back(which, d + 1, h).wait_recv()
                    tmp[h] = tmp[h] + gin[which, 2 * d + h].astype(F32)
            if d > 1:
                @pl.when(s >= d)
                def _():
                    gout[which, 2 * d + h] = tmp[h].astype(BF16)
                    back(which, d, h).start()
            else:
                for r in range(4):
                    dsend[d, 4 * h + r, which] = tmp[h, r * TOK:(r + 1) * TOK, :].astype(BF16)

    def backward(p, carry):
        i = lax.rem(j + p, KV)
        b = i // 4
        low, cotangent = plow[i], gbuf[i]
        attended = dot(vbt[b], low).astype(BF16)
        osend[i] = attended.astype(F32).T.astype(BF16)
        inner = jnp.sum(cotangent.astype(F32).T * attended.astype(F32), axis=0, keepdims=True)
        work[...] = dot(vb[b], cotangent, NT)
        factor = norm[i] * SCALE
        for n in range(ANC):
            rows = slice(n * BLK, (n + 1) * BLK)
            dlow[rows, :] = (prob[i, rows, :] * ((work[rows, :] - inner) * factor)).astype(BF16)
        dka[pl.ds(b * ANC, ANC)] += dot(dlow[...], qbuf[i]).reshape(ANC, BLK, DH)
        dqsend[i] = dot(kbt[b], dlow[...]).T.astype(BF16)

        @pl.when(i != j)
        def _():
            line_copy(4, osend.at[i], orecv.at[j], i).start()
            line_copy(5, dqsend.at[i], dqrecv.at[j], i).start()

        @pl.when(i == j)
        def _():
            orecv[j] = osend[i]
            dqrecv[j] = dqsend[i]

        return carry

    def finish(pair):
        if pair == 0:
            line_copy(4, osend.at[others], orecv.at[others], j).wait_recv()
            line_copy(5, dqsend.at[others], dqrecv.at[others], j).wait_recv()
        heads = slice(pair * 16, (pair + 1) * 16)
        x = [orecv[2 * pair + u].astype(F32).reshape(TOK, GRP, DH) for u in range(2)]
        ofin[:, heads, :] = jnp.concatenate(x, axis=1).astype(BF16)
        x = [rope_back(dqrecv[2 * pair + u].astype(F32).reshape(TOK, GRP, DH)) for u in range(2)]
        dqfin[:, heads, :] = jnp.concatenate(x, axis=1).astype(BF16)

    grad_step(1, WIN)
    last_hop(1)
    lax.fori_loop(0, 2 * ANC, values, 0)
    lax.fori_loop(1, KV // 2 + 1, backward, 0)
    grad_step(1, WIN - 1)
    lax.fori_loop(KV // 2 + 1, KV + 1, backward, 0)
    grad_step(0, WIN)
    grad_step(1, WIN - 2)
    grad_step(0, 0)
    grad_step(1, 0)

    for p in range(1, KV):
        peer = lax.rem(j + p, KV)
        line_copy(6, dsend.at[0, peer], drecv.at[0, j], peer).start()
    drecv[0, j] = dsend[0, j]

    for d in range(WIN - 1, 0, -1):
        grad_step(0, d)
        if d > 2:
            grad_step(1, d - 2)
        if d in (2, 3):
            finish(3 - d)

    @pl.when(has_left)
    def _():
        for p in range(KV):
            peer = lax.rem(j + p, KV)
            next_copy(2, 4, dsend.at[1, peer], drecv.at[1, j], left, peer).start()

    finish(2)
    finish(3)
    done = [pltpu.make_async_copy(ofin, o_out, fin.at[0]), pltpu.make_async_copy(dqfin, dq_out, fin.at[1]),
            pltpu.make_async_copy(dkfin, dk_out, fin.at[2]), pltpu.make_async_copy(dvfin, dv_out, fin.at[3])]
    done[0].start()
    done[1].start()
    line_copy(6, dsend.at[0, others], drecv.at[0, others], j).wait_recv()

    @pl.when(has_right)
    def _():
        next_copy(2, 4, dsend.at[1], drecv.at[1], right, j).wait_recv()

    @pl.when(jnp.logical_not(has_right))
    def _():
        drecv[1] = jnp.zeros_like(drecv[1])

    for which in range(2):
        for h in range(KV):
            total = drecv[0, h, which].astype(F32) + drecv[1, h, which].astype(F32)
            stage[pl.ds(h, TOK, stride=KV), :] = total
        total = stage[...].reshape(TOK, KV, DH).astype(BF16)
        if which == 0:
            dkfin[...] = rope_back(total.astype(F32)).astype(BF16)
        else:
            dvfin[...] = total
        done[2 + which].start()

    for kind, (src, dst) in enumerate((
        (ksend, ksend), (vsend, vsend), (qsend, qbuf), (gsend, gbuf), (osend, orecv), (dqsend, dqrecv),
        (dsend.at[0], drecv.at[0]),
    )):
        line_copy(kind, src.at[others], dst.at[others], j).wait_send()

    @pl.when(has_right)
    def _():
        for which in range(2):
            next_copy(which, 2 * which, slabs[which], slabs[which], right, j).wait_send()

    @pl.when(has_left)
    def _():
        next_copy(2, 4, dsend.at[1], drecv.at[1], left, j).wait_send()

    for n in range(1, WIN):
        some = pl.ds(0, 2 * n)

        @pl.when((s >= n if n == WIN - 1 else s == n) & has_right)
        def _():
            for which in range(2):
                pltpu.make_async_remote_copy(
                    src_ref=wins[which].at[some], dst_ref=wins[which].at[some], send_sem=win_s.at[which],
                    recv_sem=win_r.at[0, 0], device_id=(right, j), device_id_type=MESH,
                ).wait_send()

        @pl.when(s >= n + 1 if n == WIN - 1 else s == n + 1)
        def _():
            for which in range(2):
                pltpu.make_async_remote_copy(
                    src_ref=gout.at[which, some], dst_ref=gin.at[which, some], send_sem=grad_s.at[which],
                    recv_sem=grad_r.at[0, 0], device_id=(left, j), device_id_type=MESH,
                ).wait_send()
    for copy in done:
        copy.wait()


def copy_kernel(*refs):
    ins, outs, mids, sems = refs[:4], refs[4:8], refs[8:12], refs[12]
    first = [pltpu.make_async_copy(ins[n], mids[n], sems.at[0, n]) for n in range(4)]
    second = [pltpu.make_async_copy(mids[n], outs[n], sems.at[1, n]) for n in range(4)]
    for copy in first:
        copy.start()
    for n in range(4):
        first[n].wait()
        second[n].start()
    for copy in second:
        copy.wait()


def body(lines, q_heads, k_heads, v_heads, d_out, positions, subtree_end, ancestors):
    frequency = ROPE_BASE ** (-2.0 * (np.arange(DH) % (DH // 2)) / DH)
    frequency = jnp.asarray(frequency[None, :], F32)
    hbm = pl.BlockSpec(memory_space=pl.ANY)
    rows = pltpu.VMEM((KV, ROWS, DH), BF16)
    dma = pltpu.SemaphoreType.DMA
    shapes = tuple(jax.ShapeDtypeStruct(x.shape, BF16) for x in (q_heads, q_heads, k_heads, v_heads))
    outs = pl.pallas_call(
        functools.partial(kernel, lines),
        out_shape=shapes,
        in_specs=[hbm] * 8,
        out_specs=(hbm,) * 4,
        scratch_shapes=[
            pltpu.VMEM(q_heads.shape, BF16),
            pltpu.VMEM(k_heads.shape, BF16),
            pltpu.VMEM(k_heads.shape, BF16),
            pltpu.VMEM(q_heads.shape, BF16),
            pltpu.VMEM((1, TOK), jnp.int32),
            pltpu.VMEM((1, DH), F32),
            pltpu.SMEM((2, ANC), jnp.int32),
            pltpu.VMEM((subtree_end.shape[0] // BLK, BLK), jnp.int32),
            pltpu.VMEM((TOK, DH), F32),
            pltpu.VMEM((TOK, DH), F32),
            pltpu.VMEM((ROWS, DH), F32),
            pltpu.VMEM((KV, TOK, DH), BF16),
            pltpu.VMEM((KV, TOK, DH), BF16),
            rows, rows, rows, rows,
            pltpu.VMEM((2 * WIN, BLK, DH), BF16),
            pltpu.VMEM((2, BLK, DH), BF16),
            pltpu.VMEM((2 * WIN + 2, BLK, DH), BF16),
            pltpu.VMEM((2, KEYS, DH), BF16),
            pltpu.VMEM((2, KEYS, DH), BF16),
            pltpu.VMEM((2, DH, KEYS), BF16),
            pltpu.VMEM((2, DH, KEYS), BF16),
            pltpu.VMEM((KV, KEYS, ROWS), F32),
            pltpu.VMEM((KV, KEYS, ROWS), F32),
            pltpu.VMEM((KV, KEYS, ROWS), BF16),
            pltpu.VMEM((KEYS, ROWS), F32),
            pltpu.VMEM((KEYS, ROWS), BF16),
            pltpu.VMEM((KV, 1, ROWS), F32),
            pltpu.VMEM((2 * ANC + 1, BLK, DH), F32),
            pltpu.VMEM((2 * ANC + 1, BLK, DH), F32),
            rows, rows, rows, rows,
            pltpu.VMEM((2, BLK, DH), F32),
            pltpu.VMEM((2, 2 * WIN + 2, BLK, DH), BF16),
            pltpu.VMEM((2, 2 * WIN, BLK, DH), BF16),
            pltpu.VMEM((2, KV, 2, TOK, DH), BF16),
            pltpu.VMEM((2, KV, 2, TOK, DH), BF16),
            pltpu.VMEM(q_heads.shape, BF16),
            pltpu.VMEM(q_heads.shape, BF16),
            pltpu.VMEM(k_heads.shape, BF16),
            pltpu.VMEM(k_heads.shape, BF16),
            dma((7,)), dma((7,)),
            dma((3,)), dma((5,)),
            dma((2,)), dma((4, WIN - 1)),
            dma((2,)), dma((4, WIN - 1)),
            dma((4,)), dma((8,)),
        ],
        compiler_params=pltpu.CompilerParams(
            collective_id=0, has_side_effects=True, vmem_limit_bytes=56 << 20
        ),
        cost_estimate=pl.CostEstimate(
            flops=2 * 5 * KV * KEYS * ROWS * DH, bytes_accessed=4 << 20, transcendentals=KV * KEYS * ROWS
        ),
    )(q_heads, k_heads, v_heads, d_out, positions.reshape(1, TOK), frequency, ancestors, subtree_end.reshape(-1, BLK))
    return pl.pallas_call(
        copy_kernel,
        out_shape=shapes,
        in_specs=[hbm] * 4,
        out_specs=(hbm,) * 4,
        scratch_shapes=[pltpu.VMEM(x.shape, BF16) for x in shapes] + [dma((2, 4))],
    )(*outs)


def solution(mesh):
    token = P(("seq", "kv"), None, None)
    return jax.shard_map(
        functools.partial(body, mesh.shape["seq"]),
        mesh=mesh,
        in_specs=(token, token, token, token, P(("seq", "kv")), P(), P("seq", None)),
        out_specs=(token, token, token, token),
        check_vma=False,
    )
```

```python
import functools
import math

import jax
import jax.numpy as jnp
import numpy as np
from jax import lax
from jax.experimental import pallas as pl
from jax.experimental.pallas import tpu as pltpu
from jax.sharding import PartitionSpec as P

MESH = pl.DeviceIdType.MESH
BF16, F32 = jnp.bfloat16, jnp.float32
BLK = 128
ANC = 6
WIN = 7
KV = 8
GRP = 8
TOK = 32
DH = 128
ROWS = TOK * GRP
KEYS = ANC * BLK
ROPE_BASE = 500000.0
HIDDEN = -1e30
SCALE = 1.0 / math.sqrt(DH)
LOG2E = 1.4426950408889634
NT = (((1,), (1,)), ((), ()))
NN = (((1,), (0,)), ((), ()))


def dot(a, b, dims=NN):
    return lax.dot_general(a, b, dims, preferred_element_type=F32)


def kernel(
    lines,
    q_in, k_in, v_in, g_in, pos_in, freq_in, anc_in, end_in,
    o_out, dq_out, dk_out, dv_out,
    q_ref, k_ref, v_ref, g_ref, pos_ref, freq_ref, anc_ref, end_ref, cos_ref, sin_ref, stage, ksend, vsend, qsend, gsend, qbuf, gbuf, kwin, klast, vwin,
    kb, vb, kbt, vbt, bias, prob, plow, work, norm, dka, dva,
    osend, dqsend, orecv, dqrecv, tmp, gout, gin, dsend, drecv, ofin, dqfin, dkfin, dvfin,
    line_s, line_r, next_s, next_r, win_s, win_r, grad_s, grad_r, fin, load,
):
    s = lax.axis_index("seq")
    j = lax.axis_index("kv")
    left, right = s - 1, s + 1
    has_left, has_right = s > 0, s < lines - 1

    loads = [
        pltpu.make_async_copy(src, dst, load.at[n])
        for n, (src, dst) in enumerate((
            (v_in, v_ref), (pos_in, pos_ref), (freq_in, freq_ref), (k_in, k_ref),
            (q_in, q_ref), (g_in, g_ref), (end_in, end_ref), (anc_in, anc_ref),
        ))
    ]
    for copy in loads:
        copy.start()

    barrier = pltpu.get_barrier_semaphore()

    def greet(line, peer):
        pl.semaphore_signal(barrier, inc=1, device_id=(line, peer), device_id_type=MESH)

    for p in range(1, KV):
        greet(s, lax.rem(j + p, KV))

    @pl.when(has_left)
    def _():
        for p in range(KV):
            greet(left, lax.rem(j + p, KV))

    @pl.when(has_right)
    def _():
        for p in range(KV):
            greet(right, lax.rem(j + p, KV))

    for copy in loads[:4]:
        copy.wait()
    stage[...] = v_ref[...].astype(F32).reshape(ROWS, DH)
    for h in range(KV):
        vsend[h] = stage[pl.ds(h, TOK, stride=KV), :].astype(BF16)

    across = jnp.broadcast_to(pos_ref[...].astype(F32), (TOK, TOK))
    row = lax.broadcasted_iota(jnp.int32, (TOK, TOK), 0)
    lane = lax.broadcasted_iota(jnp.int32, (TOK, TOK), 1)
    position = jnp.sum(jnp.where(row == lane, across, 0.0), axis=1, keepdims=True)
    angle = position * freq_ref[...]
    lane = lax.broadcasted_iota(jnp.int32, (TOK, DH), 1)
    cos_ref[...] = jnp.cos(angle)
    sin_ref[...] = jnp.where(lane < DH // 2, -1.0, 1.0) * jnp.sin(angle)

    def rope(x):
        return x * cos_ref[...][:, None, :] + pltpu.roll(x, DH // 2, 2) * sin_ref[...][:, None, :]

    def rope_back(x):
        return x * cos_ref[...][:, None, :] - pltpu.roll(x, DH // 2, 2) * sin_ref[...][:, None, :]

    stage[...] = rope(k_ref[...].astype(F32)).reshape(ROWS, DH)
    for h in range(KV):
        ksend[h] = stage[pl.ds(h, TOK, stride=KV), :].astype(BF16)

    for copy in loads[4:]:
        copy.wait()

    for pair in range(KV // 2):
        x = q_ref[:, pair * 16:(pair + 1) * 16, :].astype(F32).reshape(TOK, 2, GRP, DH)
        y = g_ref[:, pair * 16:(pair + 1) * 16, :].astype(F32).reshape(TOK, 2, GRP, DH)
        for u in range(2):
            qsend[2 * pair + u] = rope(x[:, u]).reshape(ROWS, DH).astype(BF16)
            gsend[2 * pair + u] = y[:, u].reshape(ROWS, DH).astype(BF16)

    pl.semaphore_wait(
        barrier, KV - 1 + KV * has_left.astype(jnp.int32) + KV * has_right.astype(jnp.int32)
    )

    def line_copy(kind, src, dst, peer):
        return pltpu.make_async_remote_copy(
            src_ref=src, dst_ref=dst, send_sem=line_s.at[kind],
            recv_sem=line_r.at[kind], device_id=(s, peer), device_id_type=MESH,
        )

    def next_copy(kind, slot, src, dst, line, peer):
        return pltpu.make_async_remote_copy(
            src_ref=src, dst_ref=dst, send_sem=next_s.at[kind],
            recv_sem=next_r.at[slot], device_id=(line, peer), device_id_type=MESH,
        )

    others = pl.ds(0, KV - 1)

    mine = pl.ds(pl.multiple_of(lax.rem(j, 4) * TOK, TOK), TOK)

    slabs, wins = (ksend, vsend), (kwin, vwin)

    def kv_here(which, peer):
        return line_copy(which, slabs[which].at[peer], wins[which].at[j // 4, mine], peer)

    def kv_next(which, peer):
        return next_copy(
            which, 2 * which + j // 4, slabs[which].at[peer], wins[which].at[2 + j // 4, mine], right, peer
        )

    @pl.when(has_right)
    def _():
        for which in range(2):
            for p in range(KV):
                peer = lax.rem(j + p, KV)
                kv_next(which, peer).start()

    for which in range(2):
        for p in range(1, KV):
            peer = lax.rem(j + p, KV)
            kv_here(which, peer).start()
        wins[which][j // 4, mine, :] = slabs[which][j]

    for p in range(1, KV):
        peer = lax.rem(j + p, KV)
        line_copy(2, qsend.at[peer], qbuf.at[j], peer).start()
        line_copy(3, gsend.at[peer], gbuf.at[j], peer).start()
    qbuf[j] = qsend[j]
    gbuf[j] = gsend[j]

    def hop(which, d, h):
        dst = klast.at[h] if which == 0 and d == WIN else wins[which].at[2 * d + h]
        return pltpu.make_async_remote_copy(
            src_ref=wins[which].at[2 * (d - 1) + h], dst_ref=dst,
            send_sem=win_s.at[which], recv_sem=win_r.at[2 * which + h, d - 2],
            device_id=(right, j), device_id_type=MESH,
        )

    for d in range(2, WIN + 1):
        for which in range(2):
            for h in range(2):
                if d > 2:
                    @pl.when(s >= d - 1)
                    def _():
                        hop(which, d - 1, h).wait_recv()
                else:
                    @pl.when(has_left)
                    def _():
                        half = wins[which].at[2 + h]
                        next_copy(which, 2 * which + h, half, half, right, j).wait_recv()

                @pl.when((s >= d - 1) & has_right)
                def _():
                    hop(which, d, h).start()
        if d == 2:
            def mask_step(u, carry):
                b = u // ANC
                slot = lax.rem(u, ANC)
                a = anc_ref[b, slot]
                ends = end_ref[pl.ds(jnp.maximum(a, 0), 1), :].astype(F32)
                last = jnp.broadcast_to(ends, (BLK, BLK)).T
                last = jnp.where(a >= 0, last, -1.0)
                first = (a * BLK + lax.broadcasted_iota(jnp.int32, (BLK, BLK), 0)).astype(F32)
                token = lax.broadcasted_iota(jnp.int32, (BLK, BLK), 1) // GRP
                for c in range(4):
                    for half in range(2):
                        query = ((2 * s + b) * BLK + c * TOK + half * (TOK // 2) + token).astype(F32)
                        seen = (query >= first) & (query <= last)
                        bias[4 * b + c, pl.ds(pl.multiple_of(slot * BLK, BLK), BLK),
                             half * BLK:(half + 1) * BLK] = jnp.where(seen, 0.0, HIDDEN)
                return carry

            lax.fori_loop(0, 2 * ANC, mask_step, 0)
            dka[...] = jnp.zeros_like(dka)
            dva[...] = jnp.zeros_like(dva)

    def last_hop(which):
        for h in range(2):
            @pl.when(s >= WIN)
            def _():
                hop(which, WIN, h).wait_recv()

    def window_slot(b, slot):
        a = anc_ref[b, slot]
        index = 2 * (s - lax.shift_right_arithmetic(a, 1)) + (a & 1)
        return jnp.where(a >= 0, jnp.clip(index, 0, 2 * WIN + 1), 0)

    def slot_rows(slot):
        return pl.ds(pl.multiple_of(slot * BLK, BLK), BLK)

    def near_keys(u, carry):
        b, slot = u // (ANC - 2), 2 + lax.rem(u, ANC - 2)
        kb[b, slot_rows(slot), :] = kwin[jnp.minimum(window_slot(b, slot), 2 * WIN - 1)]
        return carry

    def far_keys(u, carry):
        b, slot = u // 2, lax.rem(u, 2)
        index = window_slot(b, slot)
        near = kwin[jnp.minimum(index, 2 * WIN - 1)].astype(F32)
        far = klast[jnp.maximum(index - 2 * WIN, 0)].astype(F32)
        kb[b, slot_rows(slot), :] = jnp.where(index >= 2 * WIN, far, near).astype(BF16)
        return carry

    def values(u, carry):
        b, slot = u // ANC, lax.rem(u, ANC)
        rows = slot_rows(slot)
        entry = vwin[window_slot(b, slot)]
        vb[b, rows, :] = entry
        vbt[b, :, rows] = entry.astype(F32).T.astype(BF16)
        kbt[b, :, rows] = kb[b, rows, :].astype(F32).T.astype(BF16)
        return carry

    def near_scores(p, carry):
        i = lax.rem(j + p, KV)
        prob[i, 2 * BLK:, :] = dot(kb[i // 4, 2 * BLK:, :], qbuf[i], NT)
        return carry

    for which in range(2):
        line_copy(which, slabs[which].at[others], slabs[which].at[others], j).wait_recv()
    line_copy(2, qsend.at[others], qbuf.at[others], j).wait_recv()
    lax.fori_loop(0, 2 * (ANC - 2), near_keys, 0)
    lax.fori_loop(1, KV + 1, near_scores, 0)
    line_copy(3, gsend.at[others], gbuf.at[others], j).wait_recv()
    last_hop(0)
    lax.fori_loop(0, 4, far_keys, 0)

    def forward(p, carry):
        i = lax.rem(j + p, KV)
        b = i // 4
        slots = [slice(n * BLK, (n + 1) * BLK) for n in range(ANC)]
        prob[i, :2 * BLK, :] = dot(kb[b, :2 * BLK, :], qbuf[i], NT)

        def score(n):
            return prob[i, slots[n], :] * (SCALE * LOG2E) + bias[i, slots[n], :]

        top = jnp.max(score(0), axis=0, keepdims=True)
        for n in range(1, ANC):
            top = jnp.maximum(top, jnp.max(score(n), axis=0, keepdims=True))
        total = jnp.zeros((1, ROWS), F32)
        for n in range(ANC):
            weight = jnp.exp2(score(n) - top)
            prob[i, slots[n], :] = weight
            total = total + jnp.sum(weight, axis=0, keepdims=True)
        share = 1.0 / total
        norm[i] = share
        for n in range(ANC):
            plow[i, slots[n], :] = (prob[i, slots[n], :] * share).astype(BF16)
        dva[pl.ds(b * ANC, ANC)] += dot(plow[i], gbuf[i]).reshape(ANC, BLK, DH)
        return carry

    lax.fori_loop(1, KV + 1, forward, 0)

    def back(which, d, h):
        return pltpu.make_async_remote_copy(
            src_ref=gout.at[which, 2 * d + h], dst_ref=gin.at[which, 2 * (d - 1) + h],
            send_sem=grad_s.at[which], recv_sem=grad_r.at[2 * which + h, d - 2],
            device_id=(left, j), device_id_type=MESH,
        )

    def place(b, block):
        index = 2 * ANC
        for slot in range(ANC):
            hit = (anc_ref[b, slot] == block) & (block >= 0)
            index = jnp.where(hit, b * ANC + slot, index)
        return index

    def grad_step(which, d):
        acc = (dka, dva)[which]
        for h in range(2):
            block = 2 * (s - d) + h
            tmp[h] = acc[place(0, block)] + acc[place(1, block)]
            if 0 < d < WIN:
                @pl.when((s >= d) & has_right)
                def _():
                    back(which, d + 1, h).wait_recv()
                    tmp[h] = tmp[h] + gin[which, 2 * d + h].astype(F32)
            if d > 1:
                @pl.when(s >= d)
                def _():
                    gout[which, 2 * d + h] = tmp[h].astype(BF16)
                    back(which, d, h).start()
            else:
                for r in range(4):
                    dsend[d, 4 * h + r, which] = tmp[h, r * TOK:(r + 1) * TOK, :].astype(BF16)

    def backward(p, carry):
        i = lax.rem(j + p, KV)
        b = i // 4
        low, cotangent = plow[i], gbuf[i]
        attended = dot(vbt[b], low).astype(BF16)
        osend[i] = attended.astype(F32).T.astype(BF16)
        inner = jnp.sum(cotangent.astype(F32).T * attended.astype(F32), axis=0, keepdims=True)
        work[...] = dot(vb[b], cotangent, NT)
        factor = norm[i] * SCALE
        for n in range(ANC):
            rows = slice(n * BLK, (n + 1) * BLK)
            plow[i, rows, :] = (prob[i, rows, :] * ((work[rows, :] - inner) * factor)).astype(BF16)
        dka[pl.ds(b * ANC, ANC)] += dot(plow[i], qbuf[i]).reshape(ANC, BLK, DH)

        @pl.when(i != j)
        def _():
            line_copy(4, osend.at[i], orecv.at[j], i).start()

        @pl.when(i == j)
        def _():
            orecv[j] = osend[i]

        return carry

    def query_grads(p, carry):
        i = lax.rem(j + p, KV)
        dqsend[i] = dot(kbt[i // 4], plow[i]).T.astype(BF16)

        @pl.when(i != j)
        def _():
            line_copy(5, dqsend.at[i], dqrecv.at[j], i).start()

        @pl.when(i == j)
        def _():
            dqrecv[j] = dqsend[i]

        return carry

    def finish(pair):
        if pair == 0:
            line_copy(4, osend.at[others], orecv.at[others], j).wait_recv()
            line_copy(5, dqsend.at[others], dqrecv.at[others], j).wait_recv()
        heads = slice(pair * 16, (pair + 1) * 16)
        x = [orecv[2 * pair + u].astype(F32).reshape(TOK, GRP, DH) for u in range(2)]
        ofin[:, heads, :] = jnp.concatenate(x, axis=1).astype(BF16)
        x = [rope_back(dqrecv[2 * pair + u].astype(F32).reshape(TOK, GRP, DH)) for u in range(2)]
        dqfin[:, heads, :] = jnp.concatenate(x, axis=1).astype(BF16)

    grad_step(1, WIN)
    last_hop(1)
    lax.fori_loop(0, 2 * ANC, values, 0)
    lax.fori_loop(1, KV // 2 + 1, backward, 0)
    grad_step(1, WIN - 1)
    lax.fori_loop(KV // 2 + 1, KV + 1, backward, 0)
    grad_step(0, WIN)
    grad_step(1, WIN - 2)
    grad_step(0, 0)
    grad_step(1, 0)

    for p in range(1, KV):
        peer = lax.rem(j + p, KV)
        line_copy(6, dsend.at[0, peer], drecv.at[0, j], peer).start()
    drecv[0, j] = dsend[0, j]

    for d in range(WIN - 1, 0, -1):
        grad_step(0, d)
        if d > 2:
            grad_step(1, d - 2)
        if d == WIN - 1:
            lax.fori_loop(1, KV + 1, query_grads, 0)
        if d in (2, 3):
            finish(3 - d)

    @pl.when(has_left)
    def _():
        for p in range(KV):
            peer = lax.rem(j + p, KV)
            next_copy(2, 4, dsend.at[1, peer], drecv.at[1, j], left, peer).start()

    finish(2)
    finish(3)
    done = [pltpu.make_async_copy(ofin, o_out, fin.at[0]), pltpu.make_async_copy(dqfin, dq_out, fin.at[1]),
            pltpu.make_async_copy(dkfin, dk_out, fin.at[2]), pltpu.make_async_copy(dvfin, dv_out, fin.at[3])]
    done[0].start()
    done[1].start()
    line_copy(6, dsend.at[0, others], drecv.at[0, others], j).wait_recv()

    @pl.when(has_right)
    def _():
        next_copy(2, 4, dsend.at[1], drecv.at[1], right, j).wait_recv()

    @pl.when(jnp.logical_not(has_right))
    def _():
        drecv[1] = jnp.zeros_like(drecv[1])

    for which in range(2):
        for h in range(KV):
            total = drecv[0, h, which].astype(F32) + drecv[1, h, which].astype(F32)
            stage[pl.ds(h, TOK, stride=KV), :] = total
        total = stage[...].reshape(TOK, KV, DH).astype(BF16)
        if which == 0:
            dkfin[...] = rope_back(total.astype(F32)).astype(BF16)
        else:
            dvfin[...] = total
        done[2 + which].start()

    for kind, (src, dst) in enumerate((
        (ksend, ksend), (vsend, vsend), (qsend, qbuf), (gsend, gbuf), (osend, orecv), (dqsend, dqrecv),
        (dsend.at[0], drecv.at[0]),
    )):
        line_copy(kind, src.at[others], dst.at[others], j).wait_send()

    @pl.when(has_right)
    def _():
        for which in range(2):
            next_copy(which, 2 * which, slabs[which], slabs[which], right, j).wait_send()

    @pl.when(has_left)
    def _():
        next_copy(2, 4, dsend.at[1], drecv.at[1], left, j).wait_send()

    for n in range(1, WIN):
        some = pl.ds(0, 2 * n)

        @pl.when((s >= n if n == WIN - 1 else s == n) & has_right)
        def _():
            for which in range(2):
                pltpu.make_async_remote_copy(
                    src_ref=wins[which].at[some], dst_ref=wins[which].at[some], send_sem=win_s.at[which],
                    recv_sem=win_r.at[0, 0], device_id=(right, j), device_id_type=MESH,
                ).wait_send()

        @pl.when(s >= n + 1 if n == WIN - 1 else s == n + 1)
        def _():
            for which in range(2):
                pltpu.make_async_remote_copy(
                    src_ref=gout.at[which, some], dst_ref=gin.at[which, some], send_sem=grad_s.at[which],
                    recv_sem=grad_r.at[0, 0], device_id=(left, j), device_id_type=MESH,
                ).wait_send()
    for copy in done:
        copy.wait()


def copy_kernel(*refs):
    ins, outs, mids, sems = refs[:4], refs[4:8], refs[8:12], refs[12]
    first = [pltpu.make_async_copy(ins[n], mids[n], sems.at[0, n]) for n in range(4)]
    second = [pltpu.make_async_copy(mids[n], outs[n], sems.at[1, n]) for n in range(4)]
    for copy in first:
        copy.start()
    for n in range(4):
        first[n].wait()
        second[n].start()
    for copy in second:
        copy.wait()


def body(lines, q_heads, k_heads, v_heads, d_out, positions, subtree_end, ancestors):
    frequency = ROPE_BASE ** (-2.0 * (np.arange(DH) % (DH // 2)) / DH)
    frequency = jnp.asarray(frequency[None, :], F32)
    hbm = pl.BlockSpec(memory_space=pl.ANY)
    rows = pltpu.VMEM((KV, ROWS, DH), BF16)
    dma = pltpu.SemaphoreType.DMA
    shapes = tuple(jax.ShapeDtypeStruct(x.shape, BF16) for x in (q_heads, q_heads, k_heads, v_heads))
    outs = pl.pallas_call(
        functools.partial(kernel, lines),
        out_shape=shapes,
        in_specs=[hbm] * 8,
        out_specs=(hbm,) * 4,
        scratch_shapes=[
            pltpu.VMEM(q_heads.shape, BF16),
            pltpu.VMEM(k_heads.shape, BF16),
            pltpu.VMEM(k_heads.shape, BF16),
            pltpu.VMEM(q_heads.shape, BF16),
            pltpu.VMEM((1, TOK), jnp.int32),
            pltpu.VMEM((1, DH), F32),
            pltpu.SMEM((2, ANC), jnp.int32),
            pltpu.VMEM((subtree_end.shape[0] // BLK, BLK), jnp.int32),
            pltpu.VMEM((TOK, DH), F32),
            pltpu.VMEM((TOK, DH), F32),
            pltpu.VMEM((ROWS, DH), F32),
            pltpu.VMEM((KV, TOK, DH), BF16),
            pltpu.VMEM((KV, TOK, DH), BF16),
            rows, rows, rows, rows,
            pltpu.VMEM((2 * WIN, BLK, DH), BF16),
            pltpu.VMEM((2, BLK, DH), BF16),
            pltpu.VMEM((2 * WIN + 2, BLK, DH), BF16),
            pltpu.VMEM((2, KEYS, DH), BF16),
            pltpu.VMEM((2, KEYS, DH), BF16),
            pltpu.VMEM((2, DH, KEYS), BF16),
            pltpu.VMEM((2, DH, KEYS), BF16),
            pltpu.VMEM((KV, KEYS, ROWS), F32),
            pltpu.VMEM((KV, KEYS, ROWS), F32),
            pltpu.VMEM((KV, KEYS, ROWS), BF16),
            pltpu.VMEM((KEYS, ROWS), F32),
            pltpu.VMEM((KV, 1, ROWS), F32),
            pltpu.VMEM((2 * ANC + 1, BLK, DH), F32),
            pltpu.VMEM((2 * ANC + 1, BLK, DH), F32),
            rows, rows, rows, rows,
            pltpu.VMEM((2, BLK, DH), F32),
            pltpu.VMEM((2, 2 * WIN + 2, BLK, DH), BF16),
            pltpu.VMEM((2, 2 * WIN, BLK, DH), BF16),
            pltpu.VMEM((2, KV, 2, TOK, DH), BF16),
            pltpu.VMEM((2, KV, 2, TOK, DH), BF16),
            pltpu.VMEM(q_heads.shape, BF16),
            pltpu.VMEM(q_heads.shape, BF16),
            pltpu.VMEM(k_heads.shape, BF16),
            pltpu.VMEM(k_heads.shape, BF16),
            dma((7,)), dma((7,)),
            dma((3,)), dma((5,)),
            dma((2,)), dma((4, WIN - 1)),
            dma((2,)), dma((4, WIN - 1)),
            dma((4,)), dma((8,)),
        ],
        compiler_params=pltpu.CompilerParams(
            collective_id=0, has_side_effects=True, vmem_limit_bytes=56 << 20
        ),
        cost_estimate=pl.CostEstimate(
            flops=2 * 5 * KV * KEYS * ROWS * DH, bytes_accessed=4 << 20, transcendentals=KV * KEYS * ROWS
        ),
    )(q_heads, k_heads, v_heads, d_out, positions.reshape(1, TOK), frequency, ancestors, subtree_end.reshape(-1, BLK))
    return pl.pallas_call(
        copy_kernel,
        out_shape=shapes,
        in_specs=[hbm] * 4,
        out_specs=(hbm,) * 4,
        scratch_shapes=[pltpu.VMEM(x.shape, BF16) for x in shapes] + [dma((2, 4))],
    )(*outs)


def solution(mesh):
    token = P(("seq", "kv"), None, None)
    return jax.shard_map(
        functools.partial(body, mesh.shape["seq"]),
        mesh=mesh,
        in_specs=(token, token, token, token, P(("seq", "kv")), P(), P("seq", None)),
        out_specs=(token, token, token, token),
        check_vma=False,
    )
```
